32 devices in a mesh: ctx: 4 (over x, core), tp: 8 (over z, y).
Axes of the slice: x: 2, y: 2, z: 4, core: 2. Of those that a mesh axis runs over, the one named last changes fastest.
Arguments:
- query_feats: bfloat16 [8192, 512], P('tp', 'ctx'), may hold values from -6 to 6
- key_feats: bfloat16 [8192, 512], P('tp', 'ctx'), may hold values from -6 to 6
- value_feats: bfloat16 [8192, 512], P('tp', 'ctx'), may hold values from -6 to 6
- out_gate: bfloat16 [8192, 512], P('tp', 'ctx'), may hold values from -6 to 6
- mr_filter: bfloat16 [512, 128], P('tp'), may hold values from -0.5 to 0.5
- lr_rates: float32 [512, 16], P('tp'), may hold values from 0.0009765625 to 0.1
- lr_residues: float32 [512, 16], P('tp'), may hold values from -6 to 6
- w_out: bfloat16 [8192, 8192], P('tp'), may hold values from -0.09375 to 0.09375
Outputs:
- mixed_out: bfloat16 [8192, 512], P('tp', 'ctx')
The draws below stay inside these ranges and needn't reach their ends.
All inputs are finite; a program needn't handle non-finite values.
Results may differ from the reference program's by a relative error of at most 0.023.
Values may be sent and summed in bfloat16 or wider, within the bound.
A program may use at most 128 MiB of HBM per device.

```python
import math
import jax
import jax.numpy as jnp
from jax import lax

D = 8192
MR_TAPS = 128
ORDER = 16
SEQ = 512
N_TP = 8


def strengthened(values, key, source, target, shards_of, factor):
    def block_of(position):
        return (jnp.arange(values.shape[position]) // (values.shape[position] // shards_of)).reshape((-1,) + (1,) * (values.ndim - 1 - position))

    near = jax.random.permutation(key, shards_of)[block_of(target)]
    far = (block_of(target) + shards_of // 2) % shards_of
    return jnp.where((block_of(source) == near) | (block_of(source) == far), factor * values, values)


def block_scale(key, dims, split, least, largest):
    gain = 1.0
    for position, parts in split:
        draws = jax.random.uniform(jax.random.fold_in(jax.random.fold_in(key, 6), position), (parts,), jnp.float32, least / len(split), largest / len(split))
        gain = gain * jnp.repeat(jnp.exp(draws), dims[position] // parts).reshape((-1,) + (1,) * (len(dims) - 1 - position))
    return gain


def noise(key, extent, width, bound, split=(), kind=jnp.bfloat16):
    array = width * jax.random.normal(key, extent, jnp.float32)
    if split:
        array = array * block_scale(key, extent, split, -0.22, 0.18)
    return jnp.clip(array, -bound, bound).astype(kind)


def noise_with(stream_key, shape, width, bound, cuts, heavy, dtype=jnp.bfloat16):
    drawn = width * jax.random.normal(stream_key, shape, jnp.float32)
    if cuts:
        drawn = drawn * block_scale(stream_key, shape, cuts, -0.22, 0.18)
    return jnp.clip(strengthened(drawn, jax.random.fold_in(stream_key, 3), *heavy), -bound, bound).astype(dtype)


def setup_inputs(seed: int = 0) -> dict:
    key_of = jax.random.split(jax.random.key(seed), 9)
    return {
        "query_feats": noise(key_of[0], (D, SEQ), 1.0, 6.0, ((0, 8), (1, 4))),
        "key_feats": noise(key_of[1], (D, SEQ), 1.0, 6.0, ((0, 8), (1, 4))),
        "value_feats": noise(key_of[2], (D, SEQ), 1.0, 6.0, ((0, 8), (1, 4))),
        "out_gate": noise(key_of[3], (D, SEQ), 1.0, 6.0, ((0, 8), (1, 4))),
        "mr_filter": noise(key_of[4], (D // 16, MR_TAPS), MR_TAPS ** -0.5, 0.5, ((0, 8),)),
        "lr_rates": jnp.clip(jnp.exp(math.log(0.1) - 4.6288867 * jax.random.uniform(key_of[5], (D // 16, ORDER), jnp.float32) ** block_scale(key_of[5], (D // 16, ORDER), ((0, 8),), -0.2, 0.2)), 0.0009765625, 0.1),
        "lr_residues": noise(key_of[6], (D // 16, ORDER), 1.0, 6.0, ((0, 8),), jnp.float32),
        "w_out": noise_with(key_of[7], (D, D), D ** -0.5, 0.09375, ((0, 8),), (0, 1, 8, 2.0)),
    }


def lr_filter(decay_rates, residues_in, length):
    positions = jnp.arange(length).astype(jnp.float32)
    decays = jnp.exp(-decay_rates[:, :, None] * positions[None, None, :])
    weights = residues_in * jnp.sqrt(2.0 * decay_rates / decay_rates.shape[1])
    return lax.optimization_barrier(jnp.sum(weights[:, :, None] * decays, axis=1))

def causal_conv(signal, filter_taps):
    length = signal.shape[1]
    fft_size = 2 * length
    group_count = filter_taps.shape[0]
    grouped = signal.astype(jnp.float32).reshape(group_count, -1, length)

    def convolve(pair_in):
        signal_part, taps_part = pair_in
        spectrum = jnp.fft.rfft(signal_part, n=fft_size, axis=-1)
        response = jnp.fft.rfft(taps_part, n=fft_size)
        return jnp.fft.irfft(spectrum * response[None, :], n=fft_size, axis=-1)[:, :length]
    result = lax.map(convolve, (grouped, filter_taps.astype(jnp.float32)))
    return result.reshape(signal.shape)

def reference(query_feats, key_feats, value_feats, out_gate, mr_filter, lr_rates, lr_residues, w_out):
    kv_prod = (key_feats.astype(jnp.float32) * value_feats.astype(jnp.float32)).astype(jnp.bfloat16)
    medium = causal_conv(kv_prod, mr_filter)
    gated_mid = (query_feats.astype(jnp.float32) * medium).astype(jnp.bfloat16)
    long_taps = lr_filter(lr_rates, lr_residues, SEQ)
    long_out = causal_conv(gated_mid, long_taps).astype(jnp.bfloat16)
    gated_out = (out_gate.astype(jnp.float32) * long_out.astype(jnp.float32)).astype(jnp.bfloat16)
    block_rows = D // N_TP
    gate_blocks = gated_out.reshape(N_TP, block_rows, SEQ)
    weight_blocks = w_out.reshape(N_TP, block_rows, D)

    def add_block(running, pair_in):
        gate_part, weight_part = pair_in
        partial_sum = lax.dot_general(weight_part.astype(jnp.float32), gate_part.astype(jnp.float32), (((0,), (0,)), ((), ())))
        rounded = lax.optimization_barrier(partial_sum.astype(jnp.bfloat16))
        return (running + rounded.astype(jnp.float32), None)
    running, unused = lax.scan(add_block, jnp.zeros((D, SEQ), jnp.float32), (gate_blocks, weight_blocks))
    return running.astype(jnp.bfloat16)
```

```python
import functools

import jax
import jax.numpy as jnp
from jax import lax
from jax.experimental import pallas as pl
from jax.experimental.pallas import tpu as pltpu
from jax.sharding import PartitionSpec as P

chan_group = 16
MESH = pl.DeviceIdType.MESH
HIGH = lax.Precision.HIGHEST


def dot(a, b, dims=((1,), (0,)), precision=None):
    return lax.dot_general(
        a, b, (dims, ((), ())), preferred_element_type=jnp.float32, precision=precision
    )


def iota(shape, dim):
    return lax.broadcasted_iota(jnp.int32, shape, dim)


def kernel(
    n_ctx,
    n_tp,
    q_ref,
    k_ref,
    v_ref,
    og_ref,
    mr_ref,
    rates_ref,
    res_ref,
    w_hbm,
    out_ref,
    w_ref,
    kv_ref,
    halo_ref,
    gm_ref,
    gt_ref,
    mrf_ref,
    rrow_ref,
    wrow_ref,
    med_ref,
    lng_ref,
    tail_ref,
    coef_ref,
    loc_ref,
    pack_ref,
    packf_ref,
    slot_ref,
    ysend,
    yrecv,
    acc,
    zsend,
    zrecv,
    w_sem,
    halo_send,
    halo_recv,
    st_send,
    st_recv,
    ys_sem,
    yr_sem,
    zs_sem,
    zr_sem,
):
    channels, tokens = q_ref.shape
    order = rates_ref.shape[1]
    groups = mr_ref.shape[0]
    per = tokens // order
    blocks = groups // per
    span = per * chan_group
    e_block = out_ref.shape[0]
    cw = ysend.shape[3]
    chunks = e_block // cw
    n_z = n_tp // 2
    i = lax.axis_index("ctx")
    me = lax.axis_index("tp")
    z = me // 2
    y = me % 2

    def target(p):
        q = n_z - 1 - p
        low = q - jnp.where(q <= z, 1, 0)
        high = p + jnp.where(p >= z, 1, 0)
        return jnp.where(p == n_z - 1, z, jnp.where(z < n_z // 2, low, high))

    def w_copy(b):
        cols = pl.ds(pl.multiple_of(b * e_block, e_block), e_block)
        return pltpu.make_async_copy(w_hbm.at[:, cols], w_ref.at[b], w_sem.at[b])

    @pl.loop(0, n_tp)
    def _(b):
        w_copy(b).start()

    barrier = pltpu.get_barrier_semaphore()
    for d in range(1, n_ctx):
        pl.semaphore_signal(
            barrier, inc=1, device_id={"ctx": lax.rem(i + d, n_ctx)}, device_id_type=MESH
        )
    pl.semaphore_signal(
        barrier, inc=1, device_id={"tp": z * 2 + 1 - y}, device_id_type=MESH
    )

    @pl.when(z > 0)
    def _():
        pl.semaphore_signal(barrier, inc=1, device_id={"tp": me - 2}, device_id_type=MESH)

    @pl.when(z < n_z - 1)
    def _():
        pl.semaphore_signal(barrier, inc=1, device_id={"tp": me + 2}, device_id_type=MESH)

    kv_ref[...] = (
        k_ref[...].astype(jnp.float32) * v_ref[...].astype(jnp.float32)
    ).astype(jnp.bfloat16)

    pl.semaphore_wait(
        barrier, n_ctx + jnp.where(z > 0, 1, 0) + jnp.where(z < n_z - 1, 1, 0)
    )

    halo_copy = pltpu.make_async_remote_copy(
        src_ref=kv_ref,
        dst_ref=halo_ref,
        send_sem=halo_send,
        recv_sem=halo_recv,
        device_id={"ctx": lax.rem(i + 1, n_ctx)},
        device_id_type=MESH,
    )

    @pl.when(i < n_ctx - 1)
    def _():
        halo_copy.start()

    @pl.when(i == 0)
    def _():
        halo_ref[...] = jnp.zeros_like(halo_ref)

    mrf_ref[...] = mr_ref[...].astype(jnp.float32)
    rates = rates_ref[...]
    weights = res_ref[...] * jnp.sqrt(2.0 * rates / order)
    own = iota((groups, tokens), 1) // order == iota((groups, tokens), 0) % per
    for src, dst in ((rates, rrow_ref), (weights, wrow_ref)):
        wide = jnp.where(own, jnp.concatenate([src] * per, axis=1), 0.0)
        dst[...] = jnp.sum(wide.reshape(blocks, per, tokens), axis=1)

    square = (tokens, tokens)
    row_i, col_i = iota(square, 0), iota(square, 1)
    same = row_i // chan_group == col_i // order

    @pl.loop(0, blocks)
    def _(k):
        r = rrow_ref[pl.ds(k, 1), :]
        place = row_i.astype(jnp.float32)
        exp0 = jnp.exp(-r * place)
        tail_ref[k] = jnp.exp(-r * (tokens - 1.0 - place))
        coef_ref[k] = exp0 * jnp.exp(-r)
        w_sel = jnp.where(
            iota((per, tokens), 1) // order == iota((per, tokens), 0),
            wrow_ref[pl.ds(k, 1), :],
            0.0,
        )
        taps = dot(w_sel, exp0, ((1,), (1,)), HIGH)
        mr = mrf_ref[pl.ds(pl.multiple_of(k * per, per), per), :]
        for g in range(per):
            circ = pltpu.roll(
                jnp.broadcast_to(taps[g : g + 1, :], square), 0, 1, stride=1, stride_axis=0
            )
            lng_ref[k * per + g] = jnp.where(row_i <= col_i, circ, 0.0).astype(jnp.bfloat16)
            circ = pltpu.roll(
                jnp.broadcast_to(mr[g : g + 1, :], square), 0, 1, stride=1, stride_axis=0
            )
            med_ref[k * per + g, :tokens, :] = jnp.where(row_i > col_i, circ, 0.0).astype(
                jnp.bfloat16
            )
            med_ref[k * per + g, tokens:, :] = jnp.where(row_i <= col_i, circ, 0.0).astype(
                jnp.bfloat16
            )

    packf_ref[...] = jnp.zeros_like(packf_ref)

    @pl.when(i > 0)
    def _():
        halo_copy.wait_recv()

    @pl.loop(0, blocks)
    def _(k):
        for g in range(per):
            rows = pl.ds(pl.multiple_of((k * per + g) * chan_group, chan_group), chan_group)
            signal = jnp.concatenate([halo_ref[rows, :], kv_ref[rows, :]], axis=1)
            medium = dot(signal, med_ref[k * per + g])
            gm_ref[rows, :] = (q_ref[rows, :].astype(jnp.float32) * medium).astype(jnp.bfloat16)
        rows = pl.ds(pl.multiple_of(k * span, span), span)
        state = dot(gm_ref[rows, :].astype(jnp.float32), tail_ref[k], precision=HIGH)
        state = jnp.where(same, state, 0.0).astype(jnp.bfloat16)
        spread = jnp.where(col_i == k * order + row_i % order, 1.0, 0.0).astype(jnp.bfloat16)
        packf_ref[...] += dot(state, spread)

    pack_ref[...] = packf_ref[...].astype(jnp.bfloat16)

    def st_copy(d):
        return pltpu.make_async_remote_copy(
            src_ref=pack_ref,
            dst_ref=slot_ref.at[d],
            send_sem=st_send.at[d],
            recv_sem=st_recv.at[d],
            device_id={"ctx": lax.rem(i + d + 1, n_ctx)},
            device_id_type=MESH,
        )

    @pl.loop(0, n_ctx - 1)
    def _(d):
        @pl.when(i + d + 1 < n_ctx)
        def _():
            st_copy(d).start()

        @pl.when(i < d + 1)
        def _():
            slot_ref[d] = jnp.zeros(square, jnp.bfloat16)

    @pl.loop(0, blocks)
    def _(k):
        for g in range(per):
            rows = pl.ds(pl.multiple_of((k * per + g) * chan_group, chan_group), chan_group)
            loc_ref[rows, :] = dot(gm_ref[rows, :], lng_ref[k * per + g])

    @pl.loop(0, n_ctx - 1)
    def _(d):
        @pl.when(i >= d + 1)
        def _():
            st_copy(d).wait_recv()

    @pl.loop(0, blocks)
    def _(k):
        rows = pl.ds(pl.multiple_of(k * span, span), span)
        r = rrow_ref[pl.ds(k, 1), :]
        gather = jnp.where(row_i == k * order + col_i % order, 1.0, 0.0).astype(jnp.bfloat16)

        def add(d, total):
            fade = jnp.exp(-r * (tokens * d).astype(jnp.float32))
            return total + fade * dot(slot_ref[d], gather)

        carried = lax.fori_loop(0, n_ctx - 1, add, jnp.zeros(square, jnp.float32))
        carried = jnp.where(same, carried * wrow_ref[pl.ds(k, 1), :], 0.0)
        wide = loc_ref[rows, :] + dot(carried, coef_ref[k], ((1,), (1,)), HIGH)
        gated = og_ref[rows, :].astype(jnp.float32) * wide.astype(jnp.bfloat16).astype(jnp.float32)
        gt_ref[:, rows] = gated.T.astype(jnp.bfloat16)

    @pl.loop(0, n_tp)
    def _(b):
        w_copy(b).wait()

    def y_copy(p, c):
        return pltpu.make_async_remote_copy(
            src_ref=ysend.at[p, c],
            dst_ref=yrecv.at[p, c],
            send_sem=ys_sem.at[p, c],
            recv_sem=yr_sem.at[p, c],
            device_id={"tp": z * 2 + 1 - y},
            device_id_type=MESH,
        )

    def z_copy(p, c):
        zt = target(p)
        back = jnp.where(zt < z, 1, 0)
        return pltpu.make_async_remote_copy(
            src_ref=zsend.at[p, c],
            dst_ref=zrecv.at[back, zt, c],
            send_sem=zs_sem.at[p, c],
            recv_sem=zr_sem.at[back, zt, c],
            device_id={"tp": lax.rem(me + 2 - 4 * back + n_tp, n_tp)},
            device_id_type=MESH,
        )

    def z_wait(way, zt, c):
        pltpu.make_async_remote_copy(
            src_ref=zsend.at[0, c],
            dst_ref=zrecv.at[way, zt, c],
            send_sem=zs_sem.at[0, c],
            recv_sem=zr_sem.at[way, zt, c],
            device_id={"tp": z * 2 + 1 - y},
            device_id_type=MESH,
        ).wait_recv()

    @pl.loop(0, n_z)
    def _(p):
        b = target(p) * 2 + 1 - y
        for c in range(chunks):
            ysend[p, c] = dot(gt_ref[...], w_ref[b, :, c * cw : (c + 1) * cw]).astype(jnp.bfloat16)
            y_copy(p, c).start()

    @pl.loop(0, n_z)
    def _(p):
        b = target(p) * 2 + y
        for c in range(chunks):
            acc[p, c] = dot(gt_ref[...], w_ref[b, :, c * cw : (c + 1) * cw])

    @pl.loop(0, n_z - 1)
    def _(p):
        zt = target(p)
        back = jnp.where(zt < z, 1, 0)
        joins = jnp.where(zt < z, z < n_z - 1, z > 0)

        @pl.loop(0, chunks)
        def _(c):
            y_copy(p, c).wait_recv()
            acc[p, c] += yrecv[p, c].astype(jnp.float32)

            @pl.when(joins)
            def _():
                z_wait(back, zt, c)
                acc[p, c] += zrecv[back, zt, c].astype(jnp.float32)

            zsend[p, c] = acc[p, c].astype(jnp.bfloat16)
            z_copy(p, c).start()

    for c in range(chunks):
        y_copy(n_z - 1, c).wait_recv()
        acc[n_z - 1, c] += yrecv[n_z - 1, c].astype(jnp.float32)

        @pl.when(z > 0)
        def _():
            z_wait(0, z, c)
            acc[n_z - 1, c] += zrecv[0, z, c].astype(jnp.float32)

        @pl.when(z < n_z - 1)
        def _():
            z_wait(1, z, c)
            acc[n_z - 1, c] += zrecv[1, z, c].astype(jnp.float32)

        out_ref[c * cw : (c + 1) * cw, :] = acc[n_z - 1, c].T.astype(jnp.bfloat16)

    @pl.when(i < n_ctx - 1)
    def _():
        halo_copy.wait_send()

    @pl.loop(0, n_ctx - 1)
    def _(d):
        @pl.when(i + d + 1 < n_ctx)
        def _():
            st_copy(d).wait_send()

    @pl.loop(0, n_z)
    def _(p):
        for c in range(chunks):
            y_copy(p, c).wait_send()

    @pl.loop(0, n_z - 1)
    def _(p):
        for c in range(chunks):
            z_copy(p, c).wait_send()


def per_device(n_ctx, n_tp, q, k, v, og, mr, rates, res, w):
    channels, tokens = q.shape
    groups, order = rates.shape
    assert tokens == mr.shape[1] and tokens % order == 0 and n_tp % 2 == 0
    blocks = groups * order // tokens
    e_block = w.shape[1] // n_tp
    cw = min(e_block, 256)
    chunks = e_block // cw
    n_z = n_tp // 2
    bf, f32 = jnp.bfloat16, jnp.float32
    dma = pltpu.SemaphoreType.DMA
    vmem = pl.BlockSpec(memory_space=pltpu.VMEM)
    return pl.pallas_call(
        functools.partial(kernel, n_ctx, n_tp),
        out_shape=jax.ShapeDtypeStruct((e_block, tokens), bf),
        in_specs=[vmem] * 7 + [pl.BlockSpec(memory_space=pl.ANY)],
        out_specs=vmem,
        scratch_shapes=[
            pltpu.VMEM((n_tp, channels, e_block), bf),
            pltpu.VMEM((channels, tokens), bf),
            pltpu.VMEM((channels, tokens), bf),
            pltpu.VMEM((channels, tokens), bf),
            pltpu.VMEM((tokens, channels), bf),
            pltpu.VMEM((groups, tokens), f32),
            pltpu.VMEM((blocks, tokens), f32),
            pltpu.VMEM((blocks, tokens), f32),
            pltpu.VMEM((groups, 2 * tokens, tokens), bf),
            pltpu.VMEM((groups, tokens, tokens), bf),
            pltpu.VMEM((blocks, tokens, tokens), f32),
            pltpu.VMEM((blocks, tokens, tokens), f32),
            pltpu.VMEM((channels, tokens), f32),
            pltpu.VMEM((tokens, tokens), bf),
            pltpu.VMEM((tokens, tokens), f32),
            pltpu.VMEM((n_ctx - 1, tokens, tokens), bf),
            pltpu.VMEM((n_z, chunks, tokens, cw), bf),
            pltpu.VMEM((n_z, chunks, tokens, cw), bf),
            pltpu.VMEM((n_z, chunks, tokens, cw), f32),
            pltpu.VMEM((n_z, chunks, tokens, cw), bf),
            pltpu.VMEM((2, n_z, chunks, tokens, cw), bf),
            dma((n_tp,)),
            dma,
            dma,
            dma((n_ctx - 1,)),
            dma((n_ctx - 1,)),
            dma((n_z, chunks)),
            dma((n_z, chunks)),
            dma((n_z, chunks)),
            dma((2, n_z, chunks)),
        ],
        compiler_params=pltpu.CompilerParams(
            collective_id=0, has_side_effects=True, vmem_limit_bytes=56 * 2**20
        ),
        name="conv_project",
    )(q, k, v, og, mr, rates, res, w)


def solution(mesh):
    placed = (
        P("tp", "ctx"),
        P("tp", "ctx"),
        P("tp", "ctx"),
        P("tp", "ctx"),
        P("tp", None),
        P("tp", None),
        P("tp", None),
        P("tp", None),
    )
    return jax.shard_map(
        functools.partial(per_device, mesh.shape["ctx"], mesh.shape["tp"]),
        mesh=mesh,
        in_specs=placed,
        out_specs=P("tp", "ctx"),
        check_vma=False,
    )
```

```python
import functools

import jax
import jax.numpy as jnp
from jax import lax
from jax.experimental import pallas as pl
from jax.experimental.pallas import tpu as pltpu
from jax.sharding import PartitionSpec as P

chan_group = 16
MESH = pl.DeviceIdType.MESH
HIGH = lax.Precision.HIGHEST


def dot(a, b, dims=((1,), (0,)), precision=None):
    return lax.dot_general(
        a, b, (dims, ((), ())), preferred_element_type=jnp.float32, precision=precision
    )


def upright(a, size):
    rows, cols = a.shape
    a = jnp.concatenate([a, jnp.zeros((size - rows, cols), a.dtype)], axis=0)
    a = jnp.concatenate([a, jnp.zeros((size, size - cols), a.dtype)], axis=1)
    return a.T[:cols, :rows]


def halves(a):
    high = a.astype(jnp.bfloat16)
    return high, (a - high.astype(jnp.float32)).astype(jnp.bfloat16)


def iota(shape, dim):
    return lax.broadcasted_iota(jnp.int32, shape, dim)


def kernel(
    n_ctx,
    n_tp,
    q_ref,
    k_ref,
    v_ref,
    og_ref,
    mr_ref,
    rates_ref,
    res_ref,
    w_hbm,
    out_ref,
    w_ref,
    kv_ref,
    halo_ref,
    gm_ref,
    gt_ref,
    mrf_ref,
    rrow_ref,
    wrow_ref,
    rpack_ref,
    wpack_ref,
    med_ref,
    lng_ref,
    tail_ref,
    coef_ref,
    loc_ref,
    pack_ref,
    slot_ref,
    ysend,
    yrecv,
    acc,
    zsend,
    zrecv,
    w_sem,
    halo_send,
    halo_recv,
    st_send,
    st_recv,
    ys_sem,
    yr_sem,
    zs_sem,
    zr_sem,
):
    channels, tokens = q_ref.shape
    order = rates_ref.shape[0]
    groups = mr_ref.shape[0]
    per = tokens // order
    blocks = groups // per
    span = per * chan_group
    e_block = out_ref.shape[0]
    cw = ysend.shape[3]
    chunks = e_block // cw
    n_z = n_tp // 2
    i = lax.axis_index("ctx")
    me = lax.axis_index("tp")
    z = me // 2
    y = me % 2

    def target(p):
        q = n_z - 1 - p
        low = q - jnp.where(q <= z, 1, 0)
        high = p + jnp.where(p >= z, 1, 0)
        return jnp.where(p == n_z - 1, z, jnp.where(z < n_z // 2, low, high))

    def w_copy(b):
        cols = pl.ds(pl.multiple_of(b * e_block, e_block), e_block)
        return pltpu.make_async_copy(w_hbm.at[:, cols], w_ref.at[b], w_sem.at[b])

    barrier = pltpu.get_barrier_semaphore()
    for d in range(1, n_ctx):
        pl.semaphore_signal(
            barrier, inc=1, device_id={"ctx": lax.rem(i + d, n_ctx)}, device_id_type=MESH
        )
    pl.semaphore_signal(
        barrier, inc=1, device_id={"tp": z * 2 + 1 - y}, device_id_type=MESH
    )

    @pl.when(z > 0)
    def _():
        pl.semaphore_signal(barrier, inc=1, device_id={"tp": me - 2}, device_id_type=MESH)

    @pl.when(z < n_z - 1)
    def _():
        pl.semaphore_signal(barrier, inc=1, device_id={"tp": me + 2}, device_id_type=MESH)

    kv_ref[...] = (
        k_ref[...].astype(jnp.float32) * v_ref[...].astype(jnp.float32)
    ).astype(jnp.bfloat16)

    pl.semaphore_wait(
        barrier, n_ctx + jnp.where(z > 0, 1, 0) + jnp.where(z < n_z - 1, 1, 0)
    )

    halo_copy = pltpu.make_async_remote_copy(
        src_ref=kv_ref,
        dst_ref=halo_ref,
        send_sem=halo_send,
        recv_sem=halo_recv,
        device_id={"ctx": lax.rem(i + 1, n_ctx)},
        device_id_type=MESH,
    )

    @pl.when(i < n_ctx - 1)
    def _():
        halo_copy.start()

    @pl.loop(0, n_z)
    def _(p):
        w_copy(target(p) * 2 + 1 - y).start()

    @pl.loop(0, n_z)
    def _(p):
        w_copy(target(p) * 2 + y).start()

    @pl.when(i == 0)
    def _():
        halo_ref[...] = jnp.zeros_like(halo_ref)

    mrf_ref[...] = mr_ref[...].astype(jnp.float32)
    rates = upright(rates_ref[...], tokens)
    weights = upright(res_ref[...], tokens) * jnp.sqrt(2.0 * rates / order)
    own = iota((groups, tokens), 1) // order == iota((groups, tokens), 0) % per
    for src, dst, packed in ((rates, rrow_ref, rpack_ref), (weights, wrow_ref, wpack_ref)):
        wide = jnp.where(own, jnp.concatenate([src] * per, axis=1), 0.0)
        dst[...] = jnp.sum(wide.reshape(blocks, per, tokens), axis=1)
        parts = [src[k * per : (k + 1) * per] for k in range(blocks)]
        if blocks < per:
            parts.append(jnp.zeros((per, (per - blocks) * order), jnp.float32))
        joined = jnp.concatenate(parts, axis=1)
        packed[...] = jnp.broadcast_to(
            joined[:, None, :], (per, chan_group, tokens)
        ).reshape(span, tokens)

    square = (tokens, tokens)
    row_i, col_i = iota(square, 0), iota(square, 1)
    same = row_i // chan_group == col_i // order

    @pl.loop(0, blocks, unroll=2)
    def _(k):
        r = rrow_ref[pl.ds(k, 1), :]
        place = row_i.astype(jnp.float32)
        exp0 = jnp.exp(-r * place)
        high, low = halves(jnp.exp(-r * (tokens - 1.0 - place)))
        tail_ref[k, :tokens, :] = high
        tail_ref[k, tokens:, :] = low
        high, low = halves(exp0 * jnp.exp(-r))
        coef_ref[k, :, :tokens] = high
        coef_ref[k, :, tokens : 2 * tokens] = high
        coef_ref[k, :, 2 * tokens :] = low
        w_sel = jnp.where(
            iota((per, tokens), 1) // order == iota((per, tokens), 0),
            wrow_ref[pl.ds(k, 1), :],
            0.0,
        )
        taps = dot(w_sel, exp0, ((1,), (1,)), HIGH)
        mr = mrf_ref[pl.ds(pl.multiple_of(k * per, per), per), :]
        for g in range(per):
            circ = pltpu.roll(
                jnp.broadcast_to(taps[g : g + 1, :], square), 0, 1, stride=1, stride_axis=0
            )
            lng_ref[k * per + g] = jnp.where(row_i <= col_i, circ, 0.0).astype(jnp.bfloat16)
            circ = pltpu.roll(
                jnp.broadcast_to(mr[g : g + 1, :], square), 0, 1, stride=1, stride_axis=0
            )
            med_ref[k * per + g, :tokens, :] = jnp.where(row_i > col_i, circ, 0.0).astype(
                jnp.bfloat16
            )
            med_ref[k * per + g, tokens:, :] = jnp.where(row_i <= col_i, circ, 0.0).astype(
                jnp.bfloat16
            )

    @pl.when(i > 0)
    def _():
        halo_copy.wait_recv()

    @pl.loop(0, blocks, unroll=4 if blocks % 4 == 0 else 1)
    def _(k):
        for g in range(per):
            rows = pl.ds(pl.multiple_of((k * per + g) * chan_group, chan_group), chan_group)
            signal = jnp.concatenate([halo_ref[rows, :], kv_ref[rows, :]], axis=1)
            medium = dot(signal, med_ref[k * per + g])
            gm_ref[rows, :] = (q_ref[rows, :].astype(jnp.float32) * medium).astype(jnp.bfloat16)

    packed = jnp.zeros(square, jnp.float32)
    for k in range(blocks):
        signal = gm_ref[k * span : (k + 1) * span, :]
        state = dot(jnp.concatenate([signal, signal], axis=1), tail_ref[k])
        state = jnp.where(same, state, 0.0).astype(jnp.bfloat16)
        spread = jnp.where(col_i == k * order + row_i % order, 1.0, 0.0).astype(jnp.bfloat16)
        packed += dot(state, spread)
    pack_ref[...] = packed.astype(jnp.bfloat16)

    def st_copy(d):
        return pltpu.make_async_remote_copy(
            src_ref=pack_ref,
            dst_ref=slot_ref.at[d],
            send_sem=st_send.at[d],
            recv_sem=st_recv.at[d],
            device_id={"ctx": lax.rem(i + d + 1, n_ctx)},
            device_id_type=MESH,
        )

    @pl.loop(0, n_ctx - 1)
    def _(d):
        @pl.when(i + d + 1 < n_ctx)
        def _():
            st_copy(d).start()

        @pl.when(i < d + 1)
        def _():
            slot_ref[d] = jnp.zeros(square, jnp.bfloat16)

    @pl.loop(0, blocks, unroll=4 if blocks % 4 == 0 else 1)
    def _(k):
        for g in range(per):
            rows = pl.ds(pl.multiple_of((k * per + g) * chan_group, chan_group), chan_group)
            loc_ref[rows, :] = dot(gm_ref[rows, :], lng_ref[k * per + g])

    @pl.loop(0, n_ctx - 1)
    def _(d):
        @pl.when(i >= d + 1)
        def _():
            st_copy(d).wait_recv()

    def add(d, total):
        fade = jnp.exp(-rpack_ref[...] * (tokens * d).astype(jnp.float32))
        return total + fade * slot_ref[d].astype(jnp.float32)

    carried = lax.fori_loop(0, n_ctx - 1, add, jnp.zeros(square, jnp.float32))
    carried = jnp.concatenate(halves(carried * wpack_ref[...]), axis=1)
    wide_row = iota((2 * tokens, tokens), 0) % tokens
    wide_col = iota((2 * tokens, tokens), 1)
    for k in range(blocks):
        rows = slice(k * span, (k + 1) * span)
        gather = jnp.where(wide_row == k * order + wide_col % order, 1.0, 0.0)
        modes = jnp.where(same, dot(carried, gather.astype(jnp.bfloat16)), 0.0)
        high, low = halves(modes)
        entered = dot(jnp.concatenate([high, low, high], axis=1), coef_ref[k], ((1,), (1,)))
        wide = (loc_ref[rows, :] + entered).astype(jnp.bfloat16)
        gated = og_ref[rows, :].astype(jnp.float32) * wide.astype(jnp.float32)
        gt_ref[:, rows] = gated.T.astype(jnp.bfloat16)

    def y_copy(p, c):
        return pltpu.make_async_remote_copy(
            src_ref=ysend.at[p, c],
            dst_ref=yrecv.at[p, c],
            send_sem=ys_sem.at[p, c],
            recv_sem=yr_sem.at[p, c],
            device_id={"tp": z * 2 + 1 - y},
            device_id_type=MESH,
        )

    def z_copy(p, c):
        zt = target(p)
        back = jnp.where(zt < z, 1, 0)
        return pltpu.make_async_remote_copy(
            src_ref=zsend.at[p, c],
            dst_ref=zrecv.at[back, zt, c],
            send_sem=zs_sem.at[p, c],
            recv_sem=zr_sem.at[back, zt, c],
            device_id={"tp": lax.rem(me + 2 - 4 * back + n_tp, n_tp)},
            device_id_type=MESH,
        )

    def z_wait(way, zt, c):
        pltpu.make_async_remote_copy(
            src_ref=zsend.at[0, c],
            dst_ref=zrecv.at[way, zt, c],
            send_sem=zs_sem.at[0, c],
            recv_sem=zr_sem.at[way, zt, c],
            device_id={"tp": z * 2 + 1 - y},
            device_id_type=MESH,
        ).wait_recv()

    @pl.loop(0, n_z)
    def _(p):
        b = target(p) * 2 + 1 - y
        w_copy(b).wait()
        for c in range(chunks):
            ysend[p, c] = dot(gt_ref[...], w_ref[b, :, c * cw : (c + 1) * cw]).astype(jnp.bfloat16)
            y_copy(p, c).start()

    @pl.loop(0, n_z)
    def _(p):
        b = target(p) * 2 + y
        w_copy(b).wait()
        for c in range(chunks):
            acc[p, c] = dot(gt_ref[...], w_ref[b, :, c * cw : (c + 1) * cw])

    @pl.loop(0, n_z - 1)
    def _(p):
        zt = target(p)
        back = jnp.where(zt < z, 1, 0)
        joins = jnp.where(zt < z, z < n_z - 1, z > 0)

        @pl.loop(0, chunks)
        def _(c):
            y_copy(p, c).wait_recv()
            acc[p, c] += yrecv[p, c].astype(jnp.float32)

            @pl.when(joins)
            def _():
                z_wait(back, zt, c)
                acc[p, c] += zrecv[back, zt, c].astype(jnp.float32)

            zsend[p, c] = acc[p, c].astype(jnp.bfloat16)
            z_copy(p, c).start()

    for c in range(chunks):
        y_copy(n_z - 1, c).wait_recv()
        acc[n_z - 1, c] += yrecv[n_z - 1, c].astype(jnp.float32)

        @pl.when(z > 0)
        def _():
            z_wait(0, z, c)
            acc[n_z - 1, c] += zrecv[0, z, c].astype(jnp.float32)

        @pl.when(z < n_z - 1)
        def _():
            z_wait(1, z, c)
            acc[n_z - 1, c] += zrecv[1, z, c].astype(jnp.float32)

        out_ref[c * cw : (c + 1) * cw, :] = acc[n_z - 1, c].T.astype(jnp.bfloat16)

    @pl.when(i < n_ctx - 1)
    def _():
        halo_copy.wait_send()

    @pl.loop(0, n_ctx - 1)
    def _(d):
        @pl.when(i + d + 1 < n_ctx)
        def _():
            st_copy(d).wait_send()

    @pl.loop(0, n_z)
    def _(p):
        for c in range(chunks):
            y_copy(p, c).wait_send()

    @pl.loop(0, n_z - 1)
    def _(p):
        for c in range(chunks):
            z_copy(p, c).wait_send()


def per_device(n_ctx, n_tp, q, k, v, og, mr, rates, res, w):
    channels, tokens = q.shape
    groups, order = rates.shape
    assert tokens == mr.shape[1] and tokens % order == 0 and n_tp % 2 == 0
    blocks = groups * order // tokens
    e_block = w.shape[1] // n_tp
    cw = min(e_block, 256)
    chunks = e_block // cw
    n_z = n_tp // 2
    bf, f32 = jnp.bfloat16, jnp.float32
    dma = pltpu.SemaphoreType.DMA
    vmem = pl.BlockSpec(memory_space=pltpu.VMEM)
    return pl.pallas_call(
        functools.partial(kernel, n_ctx, n_tp),
        out_shape=jax.ShapeDtypeStruct((e_block, tokens), bf),
        in_specs=[vmem] * 7 + [pl.BlockSpec(memory_space=pl.ANY)],
        out_specs=vmem,
        scratch_shapes=[
            pltpu.VMEM((n_tp, channels, e_block), bf),
            pltpu.VMEM((channels, tokens), bf),
            pltpu.VMEM((channels, tokens), bf),
            pltpu.VMEM((channels, tokens), bf),
            pltpu.VMEM((tokens, channels), bf),
            pltpu.VMEM((groups, tokens), f32),
            pltpu.VMEM((blocks, tokens), f32),
            pltpu.VMEM((blocks, tokens), f32),
            pltpu.VMEM((tokens, tokens), f32),
            pltpu.VMEM((tokens, tokens), f32),
            pltpu.VMEM((groups, 2 * tokens, tokens), bf),
            pltpu.VMEM((groups, tokens, tokens), bf),
            pltpu.VMEM((blocks, 2 * tokens, tokens), bf),
            pltpu.VMEM((blocks, tokens, 3 * tokens), bf),
            pltpu.VMEM((channels, tokens), f32),
            pltpu.VMEM((tokens, tokens), bf),
            pltpu.VMEM((n_ctx - 1, tokens, tokens), bf),
            pltpu.VMEM((n_z, chunks, tokens, cw), bf),
            pltpu.VMEM((n_z, chunks, tokens, cw), bf),
            pltpu.VMEM((n_z, chunks, tokens, cw), f32),
            pltpu.VMEM((n_z, chunks, tokens, cw), bf),
            pltpu.VMEM((2, n_z, chunks, tokens, cw), bf),
            dma((n_tp,)),
            dma,
            dma,
            dma((n_ctx - 1,)),
            dma((n_ctx - 1,)),
            dma((n_z, chunks)),
            dma((n_z, chunks)),
            dma((n_z, chunks)),
            dma((2, n_z, chunks)),
        ],
        compiler_params=pltpu.CompilerParams(
            collective_id=0, has_side_effects=True, vmem_limit_bytes=56 * 2**20
        ),
        name="conv_project",
    )(q, k, v, og, mr, rates.T, res.T, w)


def solution(mesh):
    placed = (
        P("tp", "ctx"),
        P("tp", "ctx"),
        P("tp", "ctx"),
        P("tp", "ctx"),
        P("tp", None),
        P("tp", None),
        P("tp", None),
        P("tp", None),
    )
    return jax.shard_map(
        functools.partial(per_device, mesh.shape["ctx"], mesh.shape["tp"]),
        mesh=mesh,
        in_specs=placed,
        out_specs=P("tp", "ctx"),
        check_vma=False,
    )
```

```python
import functools

import jax
import jax.numpy as jnp
from jax import lax
from jax.experimental import pallas as pl
from jax.experimental.pallas import tpu as pltpu
from jax.sharding import PartitionSpec as P

chan_group = 16
MESH = pl.DeviceIdType.MESH
HIGH = lax.Precision.HIGHEST


def dot(a, b, dims=((1,), (0,)), precision=None):
    return lax.dot_general(
        a, b, (dims, ((), ())), preferred_element_type=jnp.float32, precision=precision
    )


def upright(a, size):
    rows, cols = a.shape
    a = jnp.concatenate([a, jnp.zeros((size - rows, cols), a.dtype)], axis=0)
    a = jnp.concatenate([a, jnp.zeros((size, size - cols), a.dtype)], axis=1)
    return a.T[:cols, :rows]


def halves(a):
    high = a.astype(jnp.bfloat16)
    return high, (a - high.astype(jnp.float32)).astype(jnp.bfloat16)


def iota(shape, dim):
    return lax.broadcasted_iota(jnp.int32, shape, dim)


def kernel(
    n_ctx,
    n_tp,
    q_hbm,
    k_hbm,
    v_hbm,
    og_hbm,
    mr_ref,
    rates_ref,
    res_ref,
    w_hbm,
    out_ref,
    q_ref,
    k_ref,
    v_ref,
    og_ref,
    w_ref,
    kv_ref,
    halo_ref,
    gm_ref,
    gt_ref,
    mrf_ref,
    rrow_ref,
    wrow_ref,
    rpack_ref,
    wpack_ref,
    med_ref,
    lng_ref,
    tail_ref,
    coef_ref,
    loc_ref,
    pack_ref,
    slot_ref,
    ysend,
    yrecv,
    acc,
    zsend,
    zrecv,
    in_sem,
    w_sem,
    halo_send,
    halo_recv,
    st_send,
    st_recv,
    ys_sem,
    yr_sem,
    zs_sem,
    zr_sem,
):
    channels, tokens = q_hbm.shape
    order = rates_ref.shape[0]
    groups = mr_ref.shape[0]
    per = tokens // order
    blocks = groups // per
    span = per * chan_group
    e_block = out_ref.shape[0]
    cw = ysend.shape[3]
    chunks = e_block // cw
    half = channels // 2
    half_blocks = blocks // 2
    n_z = n_tp // 2
    i = lax.axis_index("ctx")
    me = lax.axis_index("tp")
    z = me // 2
    y = me % 2

    def target(p):
        q = n_z - 1 - p
        low = q - jnp.where(q <= z, 1, 0)
        high = p + jnp.where(p >= z, 1, 0)
        return jnp.where(p == n_z - 1, z, jnp.where(z < n_z // 2, low, high))

    def w_copy(b):
        cols = pl.ds(pl.multiple_of(b * e_block, e_block), e_block)
        return pltpu.make_async_copy(w_hbm.at[:, cols], w_ref.at[b], w_sem.at[b])

    barrier = pltpu.get_barrier_semaphore()
    for d in range(1, n_ctx):
        pl.semaphore_signal(
            barrier, inc=1, device_id={"ctx": lax.rem(i + d, n_ctx)}, device_id_type=MESH
        )
    pl.semaphore_signal(
        barrier, inc=1, device_id={"tp": z * 2 + 1 - y}, device_id_type=MESH
    )

    @pl.when(z > 0)
    def _():
        pl.semaphore_signal(barrier, inc=1, device_id={"tp": me - 2}, device_id_type=MESH)

    @pl.when(z < n_z - 1)
    def _():
        pl.semaphore_signal(barrier, inc=1, device_id={"tp": me + 2}, device_id_type=MESH)

    inputs = [
        pltpu.make_async_copy(src, dst, in_sem.at[n])
        for n, (src, dst) in enumerate(
            ((k_hbm, k_ref), (v_hbm, v_ref), (q_hbm, q_ref), (og_hbm, og_ref))
        )
    ]
    for copy in inputs:
        copy.start()

    def halo_copy(h):
        rows = pl.ds(h * half, half)
        return pltpu.make_async_remote_copy(
            src_ref=kv_ref.at[rows],
            dst_ref=halo_ref.at[rows],
            send_sem=halo_send.at[h],
            recv_sem=halo_recv.at[h],
            device_id={"ctx": lax.rem(i + 1, n_ctx)},
            device_id_type=MESH,
        )

    inputs[0].wait()
    inputs[1].wait()
    for h in range(2):
        rows = slice(h * half, (h + 1) * half)
        kv_ref[rows] = (
            k_ref[rows].astype(jnp.float32) * v_ref[rows].astype(jnp.float32)
        ).astype(jnp.bfloat16)
        if h == 0:
            pl.semaphore_wait(
                barrier, n_ctx + jnp.where(z > 0, 1, 0) + jnp.where(z < n_z - 1, 1, 0)
            )

        @pl.when(i < n_ctx - 1)
        def _():
            halo_copy(h).start()

    @pl.loop(0, n_z)
    def _(p):
        w_copy(target(p) * 2 + 1 - y).start()

    @pl.loop(0, n_z)
    def _(p):
        w_copy(target(p) * 2 + y).start()

    @pl.when(i == 0)
    def _():
        halo_ref[...] = jnp.zeros_like(halo_ref)

    mrf_ref[...] = mr_ref[...].astype(jnp.float32)
    rates = upright(rates_ref[...], tokens)
    weights = upright(res_ref[...], tokens) * jnp.sqrt(2.0 * rates / order)
    own = iota((groups, tokens), 1) // order == iota((groups, tokens), 0) % per
    for src, dst, packed in ((rates, rrow_ref, rpack_ref), (weights, wrow_ref, wpack_ref)):
        wide = jnp.where(own, jnp.concatenate([src] * per, axis=1), 0.0)
        dst[...] = jnp.sum(wide.reshape(blocks, per, tokens), axis=1)
        parts = [src[k * per : (k + 1) * per] for k in range(blocks)]
        if blocks < per:
            parts.append(jnp.zeros((per, (per - blocks) * order), jnp.float32))
        joined = jnp.concatenate(parts, axis=1)
        packed[...] = jnp.broadcast_to(
            joined[:, None, :], (per, chan_group, tokens)
        ).reshape(span, tokens)

    square = (tokens, tokens)
    row_i, col_i = iota(square, 0), iota(square, 1)
    same = row_i // chan_group == col_i // order

    @pl.loop(0, blocks, unroll=2)
    def _(k):
        r = rrow_ref[pl.ds(k, 1), :]
        place = row_i.astype(jnp.float32)
        exp0 = jnp.exp(-r * place)
        high, low = halves(jnp.exp(-r * (tokens - 1.0 - place)))
        tail_ref[k, :tokens, :] = high
        tail_ref[k, tokens:, :] = low
        high, low = halves(exp0 * jnp.exp(-r))
        coef_ref[k, :, :tokens] = high
        coef_ref[k, :, tokens : 2 * tokens] = high
        coef_ref[k, :, 2 * tokens :] = low
        w_sel = jnp.where(
            iota((per, tokens), 1) // order == iota((per, tokens), 0),
            wrow_ref[pl.ds(k, 1), :],
            0.0,
        )
        taps = dot(w_sel, exp0, ((1,), (1,)), HIGH)
        mr = mrf_ref[pl.ds(pl.multiple_of(k * per, per), per), :]
        for g in range(per):
            circ = pltpu.roll(
                jnp.broadcast_to(taps[g : g + 1, :], square), 0, 1, stride=1, stride_axis=0
            )
            lng_ref[k * per + g] = jnp.where(row_i <= col_i, circ, 0.0).astype(jnp.bfloat16)
            circ = pltpu.roll(
                jnp.broadcast_to(mr[g : g + 1, :], square), 0, 1, stride=1, stride_axis=0
            )
            med_ref[k * per + g, :tokens, :] = jnp.where(row_i > col_i, circ, 0.0).astype(
                jnp.bfloat16
            )
            med_ref[k * per + g, tokens:, :] = jnp.where(row_i <= col_i, circ, 0.0).astype(
                jnp.bfloat16
            )

    def st_copy(d, h):
        return pltpu.make_async_remote_copy(
            src_ref=pack_ref.at[h],
            dst_ref=slot_ref.at[d, h],
            send_sem=st_send.at[d, h],
            recv_sem=st_recv.at[d, h],
            device_id={"ctx": lax.rem(i + d + 1, n_ctx)},
            device_id_type=MESH,
        )

    @pl.loop(0, n_ctx - 1)
    def _(d):
        @pl.when(i < d + 1)
        def _():
            slot_ref[d] = jnp.zeros((2,) + square, jnp.bfloat16)

    inputs[2].wait()
    for h in range(2):

        @pl.when(i > 0)
        def _():
            halo_copy(h).wait_recv()

        @pl.loop(h * half_blocks, (h + 1) * half_blocks, unroll=half_blocks)
        def _(k):
            for g in range(per):
                rows = pl.ds(pl.multiple_of((k * per + g) * chan_group, chan_group), chan_group)
                signal = jnp.concatenate([halo_ref[rows, :], kv_ref[rows, :]], axis=1)
                medium = dot(signal, med_ref[k * per + g])
                gm_ref[rows, :] = (q_ref[rows, :].astype(jnp.float32) * medium).astype(
                    jnp.bfloat16
                )

        packed = jnp.zeros(square, jnp.float32)
        for k in range(h * half_blocks, (h + 1) * half_blocks):
            signal = gm_ref[k * span : (k + 1) * span, :]
            state = dot(jnp.concatenate([signal, signal], axis=1), tail_ref[k])
            state = jnp.where(same, state, 0.0).astype(jnp.bfloat16)
            spread = jnp.where(col_i == k * order + row_i % order, 1.0, 0.0)
            packed += dot(state, spread.astype(jnp.bfloat16))
        pack_ref[h] = packed.astype(jnp.bfloat16)

        @pl.loop(0, n_ctx - 1)
        def _(d):
            @pl.when(i + d + 1 < n_ctx)
            def _():
                st_copy(d, h).start()

    @pl.loop(0, blocks, unroll=4 if blocks % 4 == 0 else 1)
    def _(k):
        for g in range(per):
            rows = pl.ds(pl.multiple_of((k * per + g) * chan_group, chan_group), chan_group)
            loc_ref[rows, :] = dot(gm_ref[rows, :], lng_ref[k * per + g])

    inputs[3].wait()
    wide_row = iota((2 * tokens, tokens), 0) % tokens
    wide_col = iota((2 * tokens, tokens), 1)
    for h in range(2):

        @pl.loop(0, n_ctx - 1)
        def _(d):
            @pl.when(i >= d + 1)
            def _():
                st_copy(d, h).wait_recv()

        def add(d, total):
            fade = jnp.exp(-rpack_ref[...] * (tokens * d).astype(jnp.float32))
            return total + fade * slot_ref[d, h].astype(jnp.float32)

        carried = lax.fori_loop(0, n_ctx - 1, add, jnp.zeros(square, jnp.float32))
        carried = jnp.concatenate(halves(carried * wpack_ref[...]), axis=1)
        for k in range(h * half_blocks, (h + 1) * half_blocks):
            rows = slice(k * span, (k + 1) * span)
            gather = jnp.where(wide_row == k * order + wide_col % order, 1.0, 0.0)
            modes = jnp.where(same, dot(carried, gather.astype(jnp.bfloat16)), 0.0)
            high, low = halves(modes)
            entered = dot(jnp.concatenate([high, low, high], axis=1), coef_ref[k], ((1,), (1,)))
            wide = (loc_ref[rows, :] + entered).astype(jnp.bfloat16)
            gated = og_ref[rows, :].astype(jnp.float32) * wide.astype(jnp.float32)
            gt_ref[:, rows] = gated.T.astype(jnp.bfloat16)

    def y_copy(p, c):
        return pltpu.make_async_remote_copy(
            src_ref=ysend.at[p, c],
            dst_ref=yrecv.at[p, c],
            send_sem=ys_sem.at[p, c],
            recv_sem=yr_sem.at[p, c],
            device_id={"tp": z * 2 + 1 - y},
            device_id_type=MESH,
        )

    def z_copy(p, c):
        zt = target(p)
        back = jnp.where(zt < z, 1, 0)
        return pltpu.make_async_remote_copy(
            src_ref=zsend.at[p, c],
            dst_ref=zrecv.at[back, zt, c],
            send_sem=zs_sem.at[p, c],
            recv_sem=zr_sem.at[back, zt, c],
            device_id={"tp": lax.rem(me + 2 - 4 * back + n_tp, n_tp)},
            device_id_type=MESH,
        )

    def z_wait(way, zt, c):
        pltpu.make_async_remote_copy(
            src_ref=zsend.at[0, c],
            dst_ref=zrecv.at[way, zt, c],
            send_sem=zs_sem.at[0, c],
            recv_sem=zr_sem.at[way, zt, c],
            device_id={"tp": z * 2 + 1 - y},
            device_id_type=MESH,
        ).wait_recv()

    @pl.loop(0, n_z)
    def _(p):
        b = target(p) * 2 + 1 - y
        w_copy(b).wait()
        for c in range(chunks):
            ysend[p, c] = dot(gt_ref[...], w_ref[b, :, c * cw : (c + 1) * cw]).astype(jnp.bfloat16)
            y_copy(p, c).start()

    @pl.loop(0, n_z)
    def _(p):
        b = target(p) * 2 + y
        w_copy(b).wait()
        for c in range(chunks):
            acc[p, c] = dot(gt_ref[...], w_ref[b, :, c * cw : (c + 1) * cw])

    @pl.loop(0, n_z - 1)
    def _(p):
        zt = target(p)
        back = jnp.where(zt < z, 1, 0)
        joins = jnp.where(zt < z, z < n_z - 1, z > 0)

        @pl.loop(0, chunks)
        def _(c):
            y_copy(p, c).wait_recv()
            acc[p, c] += yrecv[p, c].astype(jnp.float32)

            @pl.when(joins)
            def _():
                z_wait(back, zt, c)
                acc[p, c] += zrecv[back, zt, c].astype(jnp.float32)

            zsend[p, c] = acc[p, c].astype(jnp.bfloat16)
            z_copy(p, c).start()

    for c in range(chunks):
        y_copy(n_z - 1, c).wait_recv()
        acc[n_z - 1, c] += yrecv[n_z - 1, c].astype(jnp.float32)

        @pl.when(z > 0)
        def _():
            z_wait(0, z, c)
            acc[n_z - 1, c] += zrecv[0, z, c].astype(jnp.float32)

        @pl.when(z < n_z - 1)
        def _():
            z_wait(1, z, c)
            acc[n_z - 1, c] += zrecv[1, z, c].astype(jnp.float32)

        out_ref[c * cw : (c + 1) * cw, :] = acc[n_z - 1, c].T.astype(jnp.bfloat16)

    @pl.when(i < n_ctx - 1)
    def _():
        for h in range(2):
            halo_copy(h).wait_send()

    @pl.loop(0, n_ctx - 1)
    def _(d):
        @pl.when(i + d + 1 < n_ctx)
        def _():
            for h in range(2):
                st_copy(d, h).wait_send()

    @pl.loop(0, n_z)
    def _(p):
        for c in range(chunks):
            y_copy(p, c).wait_send()

    @pl.loop(0, n_z - 1)
    def _(p):
        for c in range(chunks):
            z_copy(p, c).wait_send()


def per_device(n_ctx, n_tp, q, k, v, og, mr, rates, res, w):
    channels, tokens = q.shape
    groups, order = rates.shape
    assert tokens == mr.shape[1] and groups * order % (2 * tokens) == 0 and tokens % order == 0 and n_tp % 2 == 0
    blocks = groups * order // tokens
    e_block = w.shape[1] // n_tp
    cw = min(e_block, 256)
    chunks = e_block // cw
    n_z = n_tp // 2
    bf, f32 = jnp.bfloat16, jnp.float32
    dma = pltpu.SemaphoreType.DMA
    anywhere = pl.BlockSpec(memory_space=pl.ANY)
    vmem = pl.BlockSpec(memory_space=pltpu.VMEM)
    return pl.pallas_call(
        functools.partial(kernel, n_ctx, n_tp),
        out_shape=jax.ShapeDtypeStruct((e_block, tokens), bf),
        in_specs=[anywhere] * 4 + [vmem] * 3 + [anywhere],
        out_specs=vmem,
        scratch_shapes=[
            pltpu.VMEM((channels, tokens), bf),
            pltpu.VMEM((channels, tokens), bf),
            pltpu.VMEM((channels, tokens), bf),
            pltpu.VMEM((channels, tokens), bf),
            pltpu.VMEM((n_tp, channels, e_block), bf),
            pltpu.VMEM((channels, tokens), bf),
            pltpu.VMEM((channels, tokens), bf),
            pltpu.VMEM((channels, tokens), bf),
            pltpu.VMEM((tokens, channels), bf),
            pltpu.VMEM((groups, tokens), f32),
            pltpu.VMEM((blocks, tokens), f32),
            pltpu.VMEM((blocks, tokens), f32),
            pltpu.VMEM((tokens, tokens), f32),
            pltpu.VMEM((tokens, tokens), f32),
            pltpu.VMEM((groups, 2 * tokens, tokens), bf),
            pltpu.VMEM((groups, tokens, tokens), bf),
            pltpu.VMEM((blocks, 2 * tokens, tokens), bf),
            pltpu.VMEM((blocks, tokens, 3 * tokens), bf),
            pltpu.VMEM((channels, tokens), f32),
            pltpu.VMEM((2, tokens, tokens), bf),
            pltpu.VMEM((n_ctx - 1, 2, tokens, tokens), bf),
            pltpu.VMEM((n_z, chunks, tokens, cw), bf),
            pltpu.VMEM((n_z, chunks, tokens, cw), bf),
            pltpu.VMEM((n_z, chunks, tokens, cw), f32),
            pltpu.VMEM((n_z, chunks, tokens, cw), bf),
            pltpu.VMEM((2, n_z, chunks, tokens, cw), bf),
            dma((4,)),
            dma((n_tp,)),
            dma((2,)),
            dma((2,)),
            dma((n_ctx - 1, 2)),
            dma((n_ctx - 1, 2)),
            dma((n_z, chunks)),
            dma((n_z, chunks)),
            dma((n_z, chunks)),
            dma((2, n_z, chunks)),
        ],
        compiler_params=pltpu.CompilerParams(
            collective_id=0, has_side_effects=True, vmem_limit_bytes=56 * 2**20
        ),
        name="conv_project",
    )(q, k, v, og, mr, rates.T, res.T, w)


def solution(mesh):
    placed = (
        P("tp", "ctx"),
        P("tp", "ctx"),
        P("tp", "ctx"),
        P("tp", "ctx"),
        P("tp", None),
        P("tp", None),
        P("tp", None),
        P("tp", None),
    )
    return jax.shard_map(
        functools.partial(per_device, mesh.shape["ctx"], mesh.shape["tp"]),
        mesh=mesh,
        in_specs=placed,
        out_specs=P("tp", "ctx"),
        check_vma=False,
    )
```

```python
import functools

import jax
import jax.numpy as jnp
from jax import lax
from jax.experimental import pallas as pl
from jax.experimental.pallas import tpu as pltpu
from jax.sharding import PartitionSpec as P

chan_group = 16
MESH = pl.DeviceIdType.MESH
HIGH = lax.Precision.HIGHEST


def dot(a, b, dims=((1,), (0,)), precision=None):
    return lax.dot_general(
        a, b, (dims, ((), ())), preferred_element_type=jnp.float32, precision=precision
    )


def upright(a, size):
    rows, cols = a.shape
    a = jnp.concatenate([a, jnp.zeros((size - rows, cols), a.dtype)], axis=0)
    a = jnp.concatenate([a, jnp.zeros((size, size - cols), a.dtype)], axis=1)
    return a.T[:cols, :rows]


def halves(a):
    high = a.astype(jnp.bfloat16)
    return high, (a - high.astype(jnp.float32)).astype(jnp.bfloat16)


def iota(shape, dim):
    return lax.broadcasted_iota(jnp.int32, shape, dim)


def kernel(
    n_ctx,
    n_tp,
    q_hbm,
    k_hbm,
    v_hbm,
    og_hbm,
    mr_ref,
    rates_ref,
    res_ref,
    w_hbm,
    out_ref,
    q_ref,
    k_ref,
    v_ref,
    og_ref,
    w_ref,
    kv_ref,
    halo_ref,
    gm_ref,
    gt_ref,
    mrf_ref,
    rrow_ref,
    wrow_ref,
    rpack_ref,
    wpack_ref,
    med_ref,
    lng_ref,
    tail_ref,
    coef_ref,
    loc_ref,
    pack_ref,
    slot_ref,
    ysend,
    yrecv,
    acc,
    zsend,
    zrecv,
    xsend,
    xrecv,
    xacc,
    in_sem,
    w_sem,
    halo_send,
    halo_recv,
    st_send,
    st_recv,
    ys_sem,
    yr_sem,
    zs_sem,
    zr_sem,
    xs_sem,
    xr_sem,
):
    channels, tokens = q_hbm.shape
    order = rates_ref.shape[0]
    groups = mr_ref.shape[0]
    per = tokens // order
    blocks = groups // per
    span = per * chan_group
    e_block = out_ref.shape[0]
    cw = ysend.shape[3]
    chunks = e_block // cw
    first = chunks // 2
    half = channels // 2
    half_blocks = blocks // 2
    n_z = n_tp // 2
    i = lax.axis_index("ctx")
    me = lax.axis_index("tp")
    z = me // 2
    y = me % 2

    def target(p):
        t = jnp.where(z < n_z // 2, z, n_z - 1 - z)
        j = p + jnp.where(p >= jnp.where(t == 0, 1, n_z - t), 1, 0)
        s = jnp.where(j == 0, n_z - 1, jnp.where(j == 1, 0, n_z - j))
        s = jnp.where(p == n_z - 1, t, s)
        return jnp.where(z < n_z // 2, s, n_z - 1 - s)

    def w_copy(b):
        cols = pl.ds(pl.multiple_of(b * e_block, e_block), e_block)
        return pltpu.make_async_copy(w_hbm.at[:, cols], w_ref.at[b], w_sem.at[b])

    barrier = pltpu.get_barrier_semaphore()
    for d in range(1, n_ctx):
        pl.semaphore_signal(
            barrier, inc=1, device_id={"ctx": lax.rem(i + d, n_ctx)}, device_id_type=MESH
        )
    pl.semaphore_signal(
        barrier, inc=1, device_id={"tp": z * 2 + 1 - y}, device_id_type=MESH
    )

    @pl.when(z > 0)
    def _():
        pl.semaphore_signal(barrier, inc=1, device_id={"tp": me - 2}, device_id_type=MESH)

    @pl.when(z < n_z - 1)
    def _():
        pl.semaphore_signal(barrier, inc=1, device_id={"tp": me + 2}, device_id_type=MESH)

    inputs = [
        pltpu.make_async_copy(src, dst, in_sem.at[n])
        for n, (src, dst) in enumerate(
            ((k_hbm, k_ref), (v_hbm, v_ref), (q_hbm, q_ref), (og_hbm, og_ref))
        )
    ]
    for copy in inputs:
        copy.start()

    def halo_copy(h):
        rows = pl.ds(h * half, half)
        return pltpu.make_async_remote_copy(
            src_ref=kv_ref.at[rows],
            dst_ref=halo_ref.at[rows],
            send_sem=halo_send.at[h],
            recv_sem=halo_recv.at[h],
            device_id={"ctx": lax.rem(i + 1, n_ctx)},
            device_id_type=MESH,
        )

    inputs[0].wait()
    inputs[1].wait()
    for h in range(2):
        rows = slice(h * half, (h + 1) * half)
        kv_ref[rows] = (
            k_ref[rows].astype(jnp.float32) * v_ref[rows].astype(jnp.float32)
        ).astype(jnp.bfloat16)
        if h == 0:
            pl.semaphore_wait(
                barrier, n_ctx + jnp.where(z > 0, 1, 0) + jnp.where(z < n_z - 1, 1, 0)
            )

        @pl.when(i < n_ctx - 1)
        def _():
            halo_copy(h).start()

    @pl.loop(0, n_z)
    def _(p):
        w_copy(target(p) * 2 + 1 - y).start()

    @pl.loop(0, n_z)
    def _(p):
        w_copy(target(p) * 2 + y).start()

    @pl.when(i == 0)
    def _():
        halo_ref[...] = jnp.zeros_like(halo_ref)

    mrf_ref[...] = mr_ref[...].astype(jnp.float32)
    rates = upright(rates_ref[...], tokens)
    weights = upright(res_ref[...], tokens) * jnp.sqrt(2.0 * rates / order)
    own = iota((groups, tokens), 1) // order == iota((groups, tokens), 0) % per
    for src, dst, packed in ((rates, rrow_ref, rpack_ref), (weights, wrow_ref, wpack_ref)):
        wide = jnp.where(own, jnp.concatenate([src] * per, axis=1), 0.0)
        dst[...] = jnp.sum(wide.reshape(blocks, per, tokens), axis=1)
        parts = [src[k * per : (k + 1) * per] for k in range(blocks)]
        if blocks < per:
            parts.append(jnp.zeros((per, (per - blocks) * order), jnp.float32))
        joined = jnp.concatenate(parts, axis=1)
        packed[...] = jnp.broadcast_to(
            joined[:, None, :], (per, chan_group, tokens)
        ).reshape(span, tokens)

    square = (tokens, tokens)
    row_i, col_i = iota(square, 0), iota(square, 1)
    same = row_i // chan_group == col_i // order

    @pl.loop(0, blocks, unroll=2)
    def _(k):
        r = rrow_ref[pl.ds(k, 1), :]
        place = row_i.astype(jnp.float32)
        exp0 = jnp.exp(-r * place)
        high, low = halves(jnp.exp(-r * (tokens - 1.0 - place)))
        tail_ref[k, :tokens, :] = high
        tail_ref[k, tokens:, :] = low
        high, low = halves(exp0 * jnp.exp(-r))
        coef_ref[k, :, :tokens] = high
        coef_ref[k, :, tokens : 2 * tokens] = high
        coef_ref[k, :, 2 * tokens :] = low
        w_sel = jnp.where(
            iota((per, tokens), 1) // order == iota((per, tokens), 0),
            wrow_ref[pl.ds(k, 1), :],
            0.0,
        )
        taps = dot(w_sel, exp0, ((1,), (1,)), HIGH)
        mr = mrf_ref[pl.ds(pl.multiple_of(k * per, per), per), :]
        for g in range(per):
            circ = pltpu.roll(
                jnp.broadcast_to(taps[g : g + 1, :], square), 0, 1, stride=1, stride_axis=0
            )
            lng_ref[k * per + g] = jnp.where(row_i <= col_i, circ, 0.0).astype(jnp.bfloat16)
            circ = pltpu.roll(
                jnp.broadcast_to(mr[g : g + 1, :], square), 0, 1, stride=1, stride_axis=0
            )
            med_ref[k * per + g, :tokens, :] = jnp.where(row_i > col_i, circ, 0.0).astype(
                jnp.bfloat16
            )
            med_ref[k * per + g, tokens:, :] = jnp.where(row_i <= col_i, circ, 0.0).astype(
                jnp.bfloat16
            )

    def st_copy(d, h):
        return pltpu.make_async_remote_copy(
            src_ref=pack_ref.at[h],
            dst_ref=slot_ref.at[d, h],
            send_sem=st_send.at[d, h],
            recv_sem=st_recv.at[d, h],
            device_id={"ctx": lax.rem(i + d + 1, n_ctx)},
            device_id_type=MESH,
        )

    @pl.loop(0, n_ctx - 1)
    def _(d):
        @pl.when(i < d + 1)
        def _():
            slot_ref[d] = jnp.zeros((2,) + square, jnp.bfloat16)

    inputs[2].wait()
    for h in range(2):

        @pl.when(i > 0)
        def _():
            halo_copy(h).wait_recv()

        @pl.loop(h * half_blocks, (h + 1) * half_blocks, unroll=half_blocks)
        def _(k):
            for g in range(per):
                rows = pl.ds(pl.multiple_of((k * per + g) * chan_group, chan_group), chan_group)
                signal = jnp.concatenate([halo_ref[rows, :], kv_ref[rows, :]], axis=1)
                medium = dot(signal, med_ref[k * per + g])
                gm_ref[rows, :] = (q_ref[rows, :].astype(jnp.float32) * medium).astype(
                    jnp.bfloat16
                )

        packed = jnp.zeros(square, jnp.float32)
        for k in range(h * half_blocks, (h + 1) * half_blocks):
            signal = gm_ref[k * span : (k + 1) * span, :]
            state = dot(jnp.concatenate([signal, signal], axis=1), tail_ref[k])
            state = jnp.where(same, state, 0.0).astype(jnp.bfloat16)
            spread = jnp.where(col_i == k * order + row_i % order, 1.0, 0.0)
            packed += dot(state, spread.astype(jnp.bfloat16))
        pack_ref[h] = packed.astype(jnp.bfloat16)

        @pl.loop(0, n_ctx - 1)
        def _(d):
            @pl.when(i + d + 1 < n_ctx)
            def _():
                st_copy(d, h).start()

    @pl.loop(0, blocks, unroll=4 if blocks % 4 == 0 else 1)
    def _(k):
        for g in range(per):
            rows = pl.ds(pl.multiple_of((k * per + g) * chan_group, chan_group), chan_group)
            loc_ref[rows, :] = dot(gm_ref[rows, :], lng_ref[k * per + g])

    inputs[3].wait()
    wide_row = iota((2 * tokens, tokens), 0) % tokens
    wide_col = iota((2 * tokens, tokens), 1)
    for h in range(2):

        @pl.loop(0, n_ctx - 1)
        def _(d):
            @pl.when(i >= d + 1)
            def _():
                st_copy(d, h).wait_recv()

        def add(d, total):
            fade = jnp.exp(-rpack_ref[...] * (tokens * d).astype(jnp.float32))
            return total + fade * slot_ref[d, h].astype(jnp.float32)

        carried = lax.fori_loop(0, n_ctx - 1, add, jnp.zeros(square, jnp.float32))
        carried = jnp.concatenate(halves(carried * wpack_ref[...]), axis=1)
        for k in range(h * half_blocks, (h + 1) * half_blocks):
            rows = slice(k * span, (k + 1) * span)
            gather = jnp.where(wide_row == k * order + wide_col % order, 1.0, 0.0)
            modes = jnp.where(same, dot(carried, gather.astype(jnp.bfloat16)), 0.0)
            high, low = halves(modes)
            entered = dot(jnp.concatenate([high, low, high], axis=1), coef_ref[k], ((1,), (1,)))
            wide = (loc_ref[rows, :] + entered).astype(jnp.bfloat16)
            gated = og_ref[rows, :].astype(jnp.float32) * wide.astype(jnp.float32)
            gt_ref[:, rows] = gated.T.astype(jnp.bfloat16)

    def y_copy(p, c):
        return pltpu.make_async_remote_copy(
            src_ref=ysend.at[p, c],
            dst_ref=yrecv.at[p, c],
            send_sem=ys_sem.at[p, c],
            recv_sem=yr_sem.at[p, c],
            device_id={"tp": z * 2 + 1 - y},
            device_id_type=MESH,
        )

    def z_copy(p, c):
        zt = target(p)
        back = jnp.where(zt < z, 1, 0)
        return pltpu.make_async_remote_copy(
            src_ref=zsend.at[p, c],
            dst_ref=zrecv.at[back, zt, c],
            send_sem=zs_sem.at[p, c],
            recv_sem=zr_sem.at[back, zt, c],
            device_id={"tp": lax.rem(me + 2 - 4 * back + n_tp, n_tp)},
            device_id_type=MESH,
        )

    def z_wait(way, zt, c):
        pltpu.make_async_remote_copy(
            src_ref=zsend.at[0, c],
            dst_ref=zrecv.at[way, zt, c],
            send_sem=zs_sem.at[0, c],
            recv_sem=zr_sem.at[way, zt, c],
            device_id={"tp": z * 2 + 1 - y},
            device_id_type=MESH,
        ).wait_recv()

    def x_copy(p, c):
        zt = target(p)
        back = jnp.where(zt < z, 1, 0)
        end = jnp.where(zt == 0, 0, 1)
        return pltpu.make_async_remote_copy(
            src_ref=xsend.at[end, c],
            dst_ref=xrecv.at[end, c],
            send_sem=xs_sem.at[end, c],
            recv_sem=xr_sem.at[end, c],
            device_id={"tp": lax.rem(me + 2 - 4 * back + n_tp, n_tp)},
            device_id_type=MESH,
        )

    def x_wait(end, c):
        pltpu.make_async_remote_copy(
            src_ref=xsend.at[end, c],
            dst_ref=xrecv.at[end, c],
            send_sem=xs_sem.at[end, c],
            recv_sem=xr_sem.at[end, c],
            device_id={"tp": z * 2 + 1 - y},
            device_id_type=MESH,
        ).wait_recv()

    def at_end(zt):
        return jnp.logical_or(zt == 0, zt == n_z - 1)

    def send_own(p, c):
        zsend[p, c] = acc[p, c].astype(jnp.bfloat16)
        z_copy(p, c).start()

    def send_other(p, c):
        end = jnp.where(target(p) == 0, 0, 1)
        xsend[end, c] = xacc[end, c].astype(jnp.bfloat16)
        x_copy(p, c).start()

    @pl.loop(0, n_z)
    def _(p):
        zt = target(p)
        end = jnp.where(zt == 0, 0, 1)
        joins = jnp.where(zt < z, z < n_z - 1, z > 0)
        w_copy(zt * 2 + 1 - y).wait()
        w_copy(zt * 2 + y).wait()
        for c in range(chunks):
            cols = slice(c * cw, (c + 1) * cw)
            other = dot(gt_ref[...], w_ref[zt * 2 + 1 - y, :, cols])

            def across():
                ysend[p, c] = other.astype(jnp.bfloat16)
                y_copy(p, c).start()

            if c < first:

                @pl.when(at_end(zt))
                def _():
                    xacc[end, c] = other

                pl.when(jnp.logical_not(at_end(zt)))(across)
            else:
                across()
            acc[p, c] = dot(gt_ref[...], w_ref[zt * 2 + y, :, cols])
            if c < first:

                @pl.when(at_end(zt) & (zt != z) & jnp.logical_not(joins))
                def _():
                    send_own(p, c)
                    send_other(p, c)

    @pl.loop(0, n_z - 1)
    def _(p):
        zt = target(p)
        end = jnp.where(zt == 0, 0, 1)
        back = jnp.where(zt < z, 1, 0)
        joins = jnp.where(zt < z, z < n_z - 1, z > 0)

        @pl.loop(0, chunks)
        def _(c):
            ahead = at_end(zt) & (c < first)

            @pl.when(jnp.logical_not(ahead))
            def _():
                y_copy(p, c).wait_recv()
                acc[p, c] += yrecv[p, c].astype(jnp.float32)

            @pl.when(joins)
            def _():
                z_wait(back, zt, c)
                acc[p, c] += zrecv[back, zt, c].astype(jnp.float32)

            @pl.when(jnp.logical_not(ahead & jnp.logical_not(joins)))
            def _():
                send_own(p, c)

            @pl.when(ahead & joins)
            def _():
                x_wait(end, c)
                xacc[end, c] += xrecv[end, c].astype(jnp.float32)
                send_other(p, c)

    own_end = jnp.where(z == 0, 0, 1)

    @pl.when(at_end(z))
    def _():
        for c in range(first):
            x_wait(own_end, c)
            ysend[n_z - 1, c] = (
                xacc[own_end, c] + xrecv[own_end, c].astype(jnp.float32)
            ).astype(jnp.bfloat16)
            y_copy(n_z - 1, c).start()

    for c in list(range(first, chunks)) + list(range(first)):
        y_copy(n_z - 1, c).wait_recv()
        acc[n_z - 1, c] += yrecv[n_z - 1, c].astype(jnp.float32)

        @pl.when(z > 0)
        def _():
            z_wait(0, z, c)
            acc[n_z - 1, c] += zrecv[0, z, c].astype(jnp.float32)

        @pl.when(z < n_z - 1)
        def _():
            z_wait(1, z, c)
            acc[n_z - 1, c] += zrecv[1, z, c].astype(jnp.float32)

        out_ref[c * cw : (c + 1) * cw, :] = acc[n_z - 1, c].T.astype(jnp.bfloat16)

    @pl.when(i < n_ctx - 1)
    def _():
        for h in range(2):
            halo_copy(h).wait_send()

    @pl.loop(0, n_ctx - 1)
    def _(d):
        @pl.when(i + d + 1 < n_ctx)
        def _():
            for h in range(2):
                st_copy(d, h).wait_send()

    @pl.loop(0, n_z)
    def _(p):
        for c in range(chunks):
            if c < first:

                @pl.when(jnp.logical_not(at_end(target(p)) & (p < n_z - 1)))
                def _():
                    y_copy(p, c).wait_send()

                @pl.when(at_end(target(p)) & (p < n_z - 1))
                def _():
                    x_copy(p, c).wait_send()

            else:
                y_copy(p, c).wait_send()

    @pl.loop(0, n_z - 1)
    def _(p):
        for c in range(chunks):
            z_copy(p, c).wait_send()


def per_device(n_ctx, n_tp, q, k, v, og, mr, rates, res, w):
    channels, tokens = q.shape
    groups, order = rates.shape
    assert tokens == mr.shape[1] and groups * order % (2 * tokens) == 0 and tokens % order == 0 and n_tp % 2 == 0
    blocks = groups * order // tokens
    e_block = w.shape[1] // n_tp
    cw = min(e_block, 256)
    chunks = e_block // cw
    some = max(1, chunks // 2)
    n_z = n_tp // 2
    bf, f32 = jnp.bfloat16, jnp.float32
    dma = pltpu.SemaphoreType.DMA
    anywhere = pl.BlockSpec(memory_space=pl.ANY)
    vmem = pl.BlockSpec(memory_space=pltpu.VMEM)
    return pl.pallas_call(
        functools.partial(kernel, n_ctx, n_tp),
        out_shape=jax.ShapeDtypeStruct((e_block, tokens), bf),
        in_specs=[anywhere] * 4 + [vmem] * 3 + [anywhere],
        out_specs=vmem,
        scratch_shapes=[
            pltpu.VMEM((channels, tokens), bf),
            pltpu.VMEM((channels, tokens), bf),
            pltpu.VMEM((channels, tokens), bf),
            pltpu.VMEM((channels, tokens), bf),
            pltpu.VMEM((n_tp, channels, e_block), bf),
            pltpu.VMEM((channels, tokens), bf),
            pltpu.VMEM((channels, tokens), bf),
            pltpu.VMEM((channels, tokens), bf),
            pltpu.VMEM((tokens, channels), bf),
            pltpu.VMEM((groups, tokens), f32),
            pltpu.VMEM((blocks, tokens), f32),
            pltpu.VMEM((blocks, tokens), f32),
            pltpu.VMEM((tokens, tokens), f32),
            pltpu.VMEM((tokens, tokens), f32),
            pltpu.VMEM((groups, 2 * tokens, tokens), bf),
            pltpu.VMEM((groups, tokens, tokens), bf),
            pltpu.VMEM((blocks, 2 * tokens, tokens), bf),
            pltpu.VMEM((blocks, tokens, 3 * tokens), bf),
            pltpu.VMEM((channels, tokens), f32),
            pltpu.VMEM((2, tokens, tokens), bf),
            pltpu.VMEM((n_ctx - 1, 2, tokens, tokens), bf),
            pltpu.VMEM((n_z, chunks, tokens, cw), bf),
            pltpu.VMEM((n_z, chunks, tokens, cw), bf),
            pltpu.VMEM((n_z, chunks, tokens, cw), f32),
            pltpu.VMEM((n_z, chunks, tokens, cw), bf),
            pltpu.VMEM((2, n_z, chunks, tokens, cw), bf),
            pltpu.VMEM((2, some, tokens, cw), bf),
            pltpu.VMEM((2, some, tokens, cw), bf),
            pltpu.VMEM((2, some, tokens, cw), f32),
            dma((4,)),
            dma((n_tp,)),
            dma((2,)),
            dma((2,)),
            dma((n_ctx - 1, 2)),
            dma((n_ctx - 1, 2)),
            dma((n_z, chunks)),
            dma((n_z, chunks)),
            dma((n_z, chunks)),
            dma((2, n_z, chunks)),
            dma((2, some)),
            dma((2, some)),
        ],
        compiler_params=pltpu.CompilerParams(
            collective_id=0, has_side_effects=True, vmem_limit_bytes=56 * 2**20
        ),
        name="conv_project",
    )(q, k, v, og, mr, rates.T, res.T, w)


def solution(mesh):
    placed = (
        P("tp", "ctx"),
        P("tp", "ctx"),
        P("tp", "ctx"),
        P("tp", "ctx"),
        P("tp", None),
        P("tp", None),
        P("tp", None),
        P("tp", None),
    )
    return jax.shard_map(
        functools.partial(per_device, mesh.shape["ctx"], mesh.shape["tp"]),
        mesh=mesh,
        in_specs=placed,
        out_specs=P("tp", "ctx"),
        check_vma=False,
    )
```

```python
import functools

import jax
import jax.numpy as jnp
from jax import lax
from jax.experimental import pallas as pl
from jax.experimental.pallas import tpu as pltpu
from jax.sharding import PartitionSpec as P

chan_group = 16
MESH = pl.DeviceIdType.MESH


def dot(a, b, dims=((1,), (0,))):
    return lax.dot_general(a, b, (dims, ((), ())), preferred_element_type=jnp.float32)


def upright(a, size):
    rows, cols = a.shape
    a = jnp.concatenate([a, jnp.zeros((size - rows, cols), a.dtype)], axis=0)
    a = jnp.concatenate([a, jnp.zeros((size, size - cols), a.dtype)], axis=1)
    return a.T[:cols, :rows]


def halves(a):
    high = a.astype(jnp.bfloat16)
    return high, (a - high.astype(jnp.float32)).astype(jnp.bfloat16)


def iota(shape, dim):
    return lax.broadcasted_iota(jnp.int32, shape, dim)


def kernel(
    n_ctx,
    n_tp,
    q_hbm,
    k_hbm,
    v_hbm,
    og_hbm,
    mr_ref,
    rates_ref,
    res_ref,
    w_hbm,
    out_ref,
    q_ref,
    k_ref,
    v_ref,
    og_ref,
    w_ref,
    kv_ref,
    halo_ref,
    gm_ref,
    gt_ref,
    mrf_ref,
    rrow_ref,
    wrow_ref,
    rpack_ref,
    wpack_ref,
    med_ref,
    taps_ref,
    tail_ref,
    coef_ref,
    loc_ref,
    pack_ref,
    slot_ref,
    ysend,
    yrecv,
    acc,
    zsend,
    zrecv,
    xsend,
    xrecv,
    xacc,
    in_sem,
    w_sem,
    halo_send,
    halo_recv,
    st_send,
    st_recv,
    ys_sem,
    yr_sem,
    zs_sem,
    zr_sem,
    xs_sem,
    xr_sem,
):
    channels, tokens = q_hbm.shape
    order = rates_ref.shape[0]
    groups = mr_ref.shape[0]
    per = tokens // order
    blocks = groups // per
    span = per * chan_group
    e_block = out_ref.shape[0]
    cw = ysend.shape[3]
    chunks = e_block // cw
    first = chunks // 4
    half = channels // 2
    half_blocks = blocks // 2
    n_z = n_tp // 2
    i = lax.axis_index("ctx")
    me = lax.axis_index("tp")
    z = me // 2
    y = me % 2

    def target(p):
        t = jnp.where(z < n_z // 2, z, n_z - 1 - z)
        j = p + jnp.where(p >= jnp.where(t == 0, 1, n_z - t), 1, 0)
        s = jnp.where(j == 0, n_z - 1, jnp.where(j == 1, 0, n_z - j))
        s = jnp.where(p == n_z - 1, t, s)
        return jnp.where(z < n_z // 2, s, n_z - 1 - s)

    def w_copy(b):
        cols = pl.ds(pl.multiple_of(b * e_block, e_block), e_block)
        return pltpu.make_async_copy(w_hbm.at[:, cols], w_ref.at[b], w_sem.at[b])

    barrier = pltpu.get_barrier_semaphore()
    for d in range(1, n_ctx):
        pl.semaphore_signal(
            barrier, inc=1, device_id={"ctx": lax.rem(i + d, n_ctx)}, device_id_type=MESH
        )
    pl.semaphore_signal(
        barrier, inc=1, device_id={"tp": z * 2 + 1 - y}, device_id_type=MESH
    )

    @pl.when(z > 0)
    def _():
        pl.semaphore_signal(barrier, inc=1, device_id={"tp": me - 2}, device_id_type=MESH)

    @pl.when(z < n_z - 1)
    def _():
        pl.semaphore_signal(barrier, inc=1, device_id={"tp": me + 2}, device_id_type=MESH)

    inputs = [
        pltpu.make_async_copy(src, dst, in_sem.at[n])
        for n, (src, dst) in enumerate(
            ((k_hbm, k_ref), (v_hbm, v_ref), (q_hbm, q_ref), (og_hbm, og_ref))
        )
    ]
    for copy in inputs:
        copy.start()

    def halo_copy(h):
        rows = pl.ds(h * half, half)
        return pltpu.make_async_remote_copy(
            src_ref=kv_ref.at[rows],
            dst_ref=halo_ref.at[rows],
            send_sem=halo_send.at[h],
            recv_sem=halo_recv.at[h],
            device_id={"ctx": lax.rem(i + 1, n_ctx)},
            device_id_type=MESH,
        )

    inputs[0].wait()
    inputs[1].wait()
    for h in range(2):
        rows = slice(h * half, (h + 1) * half)
        kv_ref[rows] = (
            k_ref[rows].astype(jnp.float32) * v_ref[rows].astype(jnp.float32)
        ).astype(jnp.bfloat16)
        if h == 0:
            pl.semaphore_wait(
                barrier, n_ctx + jnp.where(z > 0, 1, 0) + jnp.where(z < n_z - 1, 1, 0)
            )

        @pl.when(i < n_ctx - 1)
        def _():
            halo_copy(h).start()

    @pl.loop(0, n_z)
    def _(p):
        w_copy(target(p) * 2 + 1 - y).start()

    @pl.loop(0, n_z)
    def _(p):
        w_copy(target(p) * 2 + y).start()

    @pl.when(i == 0)
    def _():
        halo_ref[...] = jnp.zeros_like(halo_ref)

    mrf_ref[...] = mr_ref[...].astype(jnp.float32)
    rates = upright(rates_ref[...], tokens)
    weights = upright(res_ref[...], tokens) * jnp.sqrt(2.0 * rates / order)
    own = iota((groups, tokens), 1) // order == iota((groups, tokens), 0) % per
    for src, dst, packed in ((rates, rrow_ref, rpack_ref), (weights, wrow_ref, wpack_ref)):
        wide = jnp.where(own, jnp.concatenate([src] * per, axis=1), 0.0)
        dst[...] = jnp.sum(wide.reshape(blocks, per, tokens), axis=1)
        parts = [src[k * per : (k + 1) * per] for k in range(blocks)]
        if blocks < per:
            parts.append(jnp.zeros((per, (per - blocks) * order), jnp.float32))
        joined = jnp.concatenate(parts, axis=1)
        packed[...] = jnp.broadcast_to(
            joined[:, None, :], (per, chan_group, tokens)
        ).reshape(span, tokens)

    square = (tokens, tokens)
    row_i, col_i = iota(square, 0), iota(square, 1)
    def around(row):
        return pltpu.roll(jnp.broadcast_to(row, square), 0, 1, stride=1, stride_axis=0)

    same = row_i // chan_group == col_i // order

    @pl.loop(0, blocks, unroll=half_blocks)
    def _(k):
        r = rrow_ref[pl.ds(k, 1), :]
        place = row_i.astype(jnp.float32)
        high, low = halves(jnp.exp(-r * (tokens - 1.0 - place)))
        tail_ref[k, :tokens, :] = high
        tail_ref[k, tokens:, :] = low
        high, low = halves(jnp.exp(-r * place))
        coef = jnp.concatenate([high, high, low], axis=1)
        coef_ref[k] = coef
        w_sel = jnp.where(
            iota((per, tokens), 1) // order == iota((per, tokens), 0),
            wrow_ref[pl.ds(k, 1), :],
            0.0,
        )
        w_high, w_low = halves(w_sel)
        group_rows = pl.ds(pl.multiple_of(k * per, per), per)
        w_parts = jnp.concatenate([w_high, w_low, w_high], axis=1)
        taps_ref[group_rows, :] = dot(w_parts, coef, ((1,), (1,)))
        mr = mrf_ref[group_rows, :]
        for g in range(per):
            circ = around(mr[g : g + 1, :])
            med_ref[k * per + g, :tokens, :] = jnp.where(row_i > col_i, circ, 0.0).astype(
                jnp.bfloat16
            )
            med_ref[k * per + g, tokens:, :] = jnp.where(row_i <= col_i, circ, 0.0).astype(
                jnp.bfloat16
            )

    def st_copy(d, h):
        return pltpu.make_async_remote_copy(
            src_ref=pack_ref.at[h],
            dst_ref=slot_ref.at[d, h],
            send_sem=st_send.at[d, h],
            recv_sem=st_recv.at[d, h],
            device_id={"ctx": lax.rem(i + d + 1, n_ctx)},
            device_id_type=MESH,
        )

    @pl.loop(0, n_ctx - 1)
    def _(d):
        @pl.when(i < d + 1)
        def _():
            slot_ref[d] = jnp.zeros((2,) + square, jnp.bfloat16)

    inputs[2].wait()
    for h in range(2):

        @pl.when(i > 0)
        def _():
            halo_copy(h).wait_recv()

        @pl.loop(h * half_blocks, (h + 1) * half_blocks, unroll=half_blocks)
        def _(k):
            for g in range(per):
                rows = pl.ds(pl.multiple_of((k * per + g) * chan_group, chan_group), chan_group)
                signal = jnp.concatenate([halo_ref[rows, :], kv_ref[rows, :]], axis=1)
                medium = dot(signal, med_ref[k * per + g])
                gm_ref[rows, :] = (q_ref[rows, :].astype(jnp.float32) * medium).astype(
                    jnp.bfloat16
                )

        packed = jnp.zeros(square, jnp.float32)
        for k in range(h * half_blocks, (h + 1) * half_blocks):
            signal = gm_ref[k * span : (k + 1) * span, :]
            state = dot(jnp.concatenate([signal, signal], axis=1), tail_ref[k])
            state = jnp.where(same, state, 0.0).astype(jnp.bfloat16)
            spread = jnp.where(col_i == k * order + row_i % order, 1.0, 0.0)
            packed += dot(state, spread.astype(jnp.bfloat16))
        pack_ref[h] = packed.astype(jnp.bfloat16)

        @pl.loop(0, n_ctx - 1)
        def _(d):
            @pl.when(i + d + 1 < n_ctx)
            def _():
                st_copy(d, h).start()

    @pl.loop(0, blocks, unroll=half_blocks)
    def _(k):
        taps = taps_ref[pl.ds(pl.multiple_of(k * per, per), per), :]
        for g in range(per):
            rows = pl.ds(pl.multiple_of((k * per + g) * chan_group, chan_group), chan_group)
            circ = jnp.where(row_i <= col_i, around(taps[g : g + 1, :]), 0.0)
            loc_ref[rows, :] = dot(gm_ref[rows, :], circ.astype(jnp.bfloat16))

    inputs[3].wait()
    wide_row = iota((2 * tokens, tokens), 0) % tokens
    wide_col = iota((2 * tokens, tokens), 1)
    for h in range(2):

        @pl.loop(0, n_ctx - 1)
        def _(d):
            @pl.when(i >= d + 1)
            def _():
                st_copy(d, h).wait_recv()

        def add(d, total):
            fade = jnp.exp(-rpack_ref[...] * (tokens * d + 1).astype(jnp.float32))
            return total + fade * slot_ref[d, h].astype(jnp.float32)

        carried = lax.fori_loop(0, n_ctx - 1, add, jnp.zeros(square, jnp.float32))
        carried = jnp.concatenate(halves(carried * wpack_ref[...]), axis=1)
        for k in range(h * half_blocks, (h + 1) * half_blocks):
            rows = slice(k * span, (k + 1) * span)
            gather = jnp.where(wide_row == k * order + wide_col % order, 1.0, 0.0)
            modes = jnp.where(same, dot(carried, gather.astype(jnp.bfloat16)), 0.0)
            high, low = halves(modes)
            entered = dot(jnp.concatenate([high, low, high], axis=1), coef_ref[k], ((1,), (1,)))
            wide = (loc_ref[rows, :] + entered).astype(jnp.bfloat16)
            gated = og_ref[rows, :].astype(jnp.float32) * wide.astype(jnp.float32)
            gt_ref[:, rows] = gated.T.astype(jnp.bfloat16)

    def y_copy(p, c):
        return pltpu.make_async_remote_copy(
            src_ref=ysend.at[p, c],
            dst_ref=yrecv.at[p, c],
            send_sem=ys_sem.at[p, c],
            recv_sem=yr_sem.at[p, c],
            device_id={"tp": z * 2 + 1 - y},
            device_id_type=MESH,
        )

    def z_copy(p, c):
        zt = target(p)
        back = jnp.where(zt < z, 1, 0)
        return pltpu.make_async_remote_copy(
            src_ref=zsend.at[p, c],
            dst_ref=zrecv.at[back, zt, c],
            send_sem=zs_sem.at[p, c],
            recv_sem=zr_sem.at[back, zt, c],
            device_id={"tp": lax.rem(me + 2 - 4 * back + n_tp, n_tp)},
            device_id_type=MESH,
        )

    def z_wait(way, zt, c):
        pltpu.make_async_remote_copy(
            src_ref=zsend.at[0, c],
            dst_ref=zrecv.at[way, zt, c],
            send_sem=zs_sem.at[0, c],
            recv_sem=zr_sem.at[way, zt, c],
            device_id={"tp": z * 2 + 1 - y},
            device_id_type=MESH,
        ).wait_recv()

    def x_copy(p, c):
        zt = target(p)
        back = jnp.where(zt < z, 1, 0)
        end = jnp.where(zt == 0, 0, 1)
        return pltpu.make_async_remote_copy(
            src_ref=xsend.at[end, c],
            dst_ref=xrecv.at[end, c],
            send_sem=xs_sem.at[end, c],
            recv_sem=xr_sem.at[end, c],
            device_id={"tp": lax.rem(me + 2 - 4 * back + n_tp, n_tp)},
            device_id_type=MESH,
        )

    def x_wait(end, c):
        pltpu.make_async_remote_copy(
            src_ref=xsend.at[end, c],
            dst_ref=xrecv.at[end, c],
            send_sem=xs_sem.at[end, c],
            recv_sem=xr_sem.at[end, c],
            device_id={"tp": z * 2 + 1 - y},
            device_id_type=MESH,
        ).wait_recv()

    def at_end(zt):
        return jnp.logical_or(zt == 0, zt == n_z - 1)

    def send_own(p, c):
        zsend[p, c] = acc[p, c].astype(jnp.bfloat16)
        z_copy(p, c).start()

    def send_other(p, c):
        end = jnp.where(target(p) == 0, 0, 1)
        xsend[end, c] = xacc[end, c].astype(jnp.bfloat16)
        x_copy(p, c).start()

    @pl.loop(0, n_z)
    def _(p):
        zt = target(p)
        end = jnp.where(zt == 0, 0, 1)
        joins = jnp.where(zt < z, z < n_z - 1, z > 0)
        w_copy(zt * 2 + 1 - y).wait()
        w_copy(zt * 2 + y).wait()
        for c in range(chunks):
            cols = slice(c * cw, (c + 1) * cw)
            other = dot(gt_ref[...], w_ref[zt * 2 + 1 - y, :, cols])

            def across():
                ysend[p, c] = other.astype(jnp.bfloat16)
                y_copy(p, c).start()

            if c < first:

                @pl.when(at_end(zt))
                def _():
                    xacc[end, c] = other

                pl.when(jnp.logical_not(at_end(zt)))(across)
            else:
                across()
            acc[p, c] = dot(gt_ref[...], w_ref[zt * 2 + y, :, cols])
            if c < first:

                @pl.when(at_end(zt) & (zt != z) & jnp.logical_not(joins))
                def _():
                    send_own(p, c)
                    send_other(p, c)

    @pl.loop(0, n_z - 1)
    def _(p):
        zt = target(p)
        end = jnp.where(zt == 0, 0, 1)
        back = jnp.where(zt < z, 1, 0)
        joins = jnp.where(zt < z, z < n_z - 1, z > 0)

        @pl.loop(0, chunks)
        def _(c):
            ahead = at_end(zt) & (c < first)

            @pl.when(jnp.logical_not(ahead))
            def _():
                y_copy(p, c).wait_recv()
                acc[p, c] += yrecv[p, c].astype(jnp.float32)

            @pl.when(joins)
            def _():
                z_wait(back, zt, c)
                acc[p, c] += zrecv[back, zt, c].astype(jnp.float32)

            @pl.when(jnp.logical_not(ahead & jnp.logical_not(joins)))
            def _():
                send_own(p, c)

            @pl.when(ahead & joins)
            def _():
                x_wait(end, c)
                xacc[end, c] += xrecv[end, c].astype(jnp.float32)
                send_other(p, c)

    own_end = jnp.where(z == 0, 0, 1)

    @pl.when(at_end(z))
    def _():
        for c in range(first):
            x_wait(own_end, c)
            ysend[n_z - 1, c] = (
                xacc[own_end, c] + xrecv[own_end, c].astype(jnp.float32)
            ).astype(jnp.bfloat16)
            y_copy(n_z - 1, c).start()

    for c in list(range(first, chunks)) + list(range(first)):
        y_copy(n_z - 1, c).wait_recv()
        acc[n_z - 1, c] += yrecv[n_z - 1, c].astype(jnp.float32)

        @pl.when(z > 0)
        def _():
            z_wait(0, z, c)
            acc[n_z - 1, c] += zrecv[0, z, c].astype(jnp.float32)

        @pl.when(z < n_z - 1)
        def _():
            z_wait(1, z, c)
            acc[n_z - 1, c] += zrecv[1, z, c].astype(jnp.float32)

        out_ref[c * cw : (c + 1) * cw, :] = acc[n_z - 1, c].T.astype(jnp.bfloat16)

    @pl.when(i < n_ctx - 1)
    def _():
        for h in range(2):
            halo_copy(h).wait_send()

    @pl.loop(0, n_ctx - 1)
    def _(d):
        @pl.when(i + d + 1 < n_ctx)
        def _():
            for h in range(2):
                st_copy(d, h).wait_send()

    @pl.loop(0, n_z)
    def _(p):
        for c in range(chunks):
            if c < first:

                @pl.when(jnp.logical_not(at_end(target(p)) & (p < n_z - 1)))
                def _():
                    y_copy(p, c).wait_send()

                @pl.when(at_end(target(p)) & (p < n_z - 1))
                def _():
                    x_copy(p, c).wait_send()

            else:
                y_copy(p, c).wait_send()

    @pl.loop(0, n_z - 1)
    def _(p):
        for c in range(chunks):
            z_copy(p, c).wait_send()


def per_device(n_ctx, n_tp, q, k, v, og, mr, rates, res, w):
    channels, tokens = q.shape
    groups, order = rates.shape
    assert tokens == mr.shape[1] and groups * order % (2 * tokens) == 0 and tokens % order == 0 and n_tp % 2 == 0
    blocks = groups * order // tokens
    e_block = w.shape[1] // n_tp
    cw = min(e_block, 256)
    chunks = e_block // cw
    some = max(1, chunks // 4)
    n_z = n_tp // 2
    bf, f32 = jnp.bfloat16, jnp.float32
    dma = pltpu.SemaphoreType.DMA
    anywhere = pl.BlockSpec(memory_space=pl.ANY)
    vmem = pl.BlockSpec(memory_space=pltpu.VMEM)
    return pl.pallas_call(
        functools.partial(kernel, n_ctx, n_tp),
        out_shape=jax.ShapeDtypeStruct((e_block, tokens), bf),
        in_specs=[anywhere] * 4 + [vmem] * 3 + [anywhere],
        out_specs=vmem,
        scratch_shapes=[
            pltpu.VMEM((channels, tokens), bf),
            pltpu.VMEM((channels, tokens), bf),
            pltpu.VMEM((channels, tokens), bf),
            pltpu.VMEM((channels, tokens), bf),
            pltpu.VMEM((n_tp, channels, e_block), bf),
            pltpu.VMEM((channels, tokens), bf),
            pltpu.VMEM((channels, tokens), bf),
            pltpu.VMEM((channels, tokens), bf),
            pltpu.VMEM((tokens, channels), bf),
            pltpu.VMEM((groups, tokens), f32),
            pltpu.VMEM((blocks, tokens), f32),
            pltpu.VMEM((blocks, tokens), f32),
            pltpu.VMEM((tokens, tokens), f32),
            pltpu.VMEM((tokens, tokens), f32),
            pltpu.VMEM((groups, 2 * tokens, tokens), bf),
            pltpu.VMEM((groups, tokens), f32),
            pltpu.VMEM((blocks, 2 * tokens, tokens), bf),
            pltpu.VMEM((blocks, tokens, 3 * tokens), bf),
            pltpu.VMEM((channels, tokens), f32),
            pltpu.VMEM((2, tokens, tokens), bf),
            pltpu.VMEM((n_ctx - 1, 2, tokens, tokens), bf),
            pltpu.VMEM((n_z, chunks, tokens, cw), bf),
            pltpu.VMEM((n_z, chunks, tokens, cw), bf),
            pltpu.VMEM((n_z, chunks, tokens, cw), f32),
            pltpu.VMEM((n_z, chunks, tokens, cw), bf),
            pltpu.VMEM((2, n_z, chunks, tokens, cw), bf),
            pltpu.VMEM((2, some, tokens, cw), bf),
            pltpu.VMEM((2, some, tokens, cw), bf),
            pltpu.VMEM((2, some, tokens, cw), f32),
            dma((4,)),
            dma((n_tp,)),
            dma((2,)),
            dma((2,)),
            dma((n_ctx - 1, 2)),
            dma((n_ctx - 1, 2)),
            dma((n_z, chunks)),
            dma((n_z, chunks)),
            dma((n_z, chunks)),
            dma((2, n_z, chunks)),
            dma((2, some)),
            dma((2, some)),
        ],
        compiler_params=pltpu.CompilerParams(
            collective_id=0, has_side_effects=True, vmem_limit_bytes=56 * 2**20
        ),
        name="conv_project",
    )(q, k, v, og, mr, rates.T, res.T, w)


def solution(mesh):
    placed = (
        P("tp", "ctx"),
        P("tp", "ctx"),
        P("tp", "ctx"),
        P("tp", "ctx"),
        P("tp", None),
        P("tp", None),
        P("tp", None),
        P("tp", None),
    )
    return jax.shard_map(
        functools.partial(per_device, mesh.shape["ctx"], mesh.shape["tp"]),
        mesh=mesh,
        in_specs=placed,
        out_specs=P("tp", "ctx"),
        check_vma=False,
    )
```

```python
import functools

import jax
import jax.numpy as jnp
from jax import lax
from jax.experimental import pallas as pl
from jax.experimental.pallas import tpu as pltpu
from jax.sharding import PartitionSpec as P

chan_group = 16
MESH = pl.DeviceIdType.MESH


def dot(a, b, dims=((1,), (0,))):
    return lax.dot_general(a, b, (dims, ((), ())), preferred_element_type=jnp.float32)


def upright(a, size):
    rows, cols = a.shape
    a = jnp.concatenate([a, jnp.zeros((size - rows, cols), a.dtype)], axis=0)
    a = jnp.concatenate([a, jnp.zeros((size, size - cols), a.dtype)], axis=1)
    return a.T[:cols, :rows]


def halves(a):
    high = a.astype(jnp.bfloat16)
    return high, (a - high.astype(jnp.float32)).astype(jnp.bfloat16)


def iota(shape, dim):
    return lax.broadcasted_iota(jnp.int32, shape, dim)


def kernel(
    n_ctx,
    n_tp,
    q_hbm,
    k_hbm,
    v_hbm,
    og_hbm,
    mr_ref,
    rates_ref,
    res_ref,
    w_hbm,
    out_ref,
    q_ref,
    k_ref,
    v_ref,
    og_ref,
    w_ref,
    kv_ref,
    halo_ref,
    gm_ref,
    gt_ref,
    mrf_ref,
    rrow_ref,
    wrow_ref,
    rpack_ref,
    wpack_ref,
    med_ref,
    taps_ref,
    tail_ref,
    coef_ref,
    loc_ref,
    pack_ref,
    slot_ref,
    ysend,
    yrecv,
    acc,
    zsend,
    zrecv,
    xsend,
    xrecv,
    xacc,
    in_sem,
    w_sem,
    halo_send,
    halo_recv,
    st_send,
    st_recv,
    ys_sem,
    yr_sem,
    zs_sem,
    zr_sem,
    xs_sem,
    xr_sem,
):
    channels, tokens = q_hbm.shape
    order = rates_ref.shape[0]
    groups = mr_ref.shape[0]
    per = tokens // order
    blocks = groups // per
    span = per * chan_group
    e_block = out_ref.shape[0]
    cw = ysend.shape[3]
    chunks = e_block // cw
    first = chunks // 4
    half = channels // 2
    half_blocks = blocks // 2
    n_z = n_tp // 2
    i = lax.axis_index("ctx")
    me = lax.axis_index("tp")
    z = me // 2
    y = me % 2

    def target(p):
        t = jnp.where(z < n_z // 2, z, n_z - 1 - z)
        j = p + jnp.where(p >= jnp.where(t == 0, 1, n_z - t), 1, 0)
        s = jnp.where(j == 0, n_z - 1, jnp.where(j == 1, 0, n_z - j))
        s = jnp.where(p == n_z - 1, t, s)
        return jnp.where(z < n_z // 2, s, n_z - 1 - s)

    def w_copy(b):
        cols = pl.ds(pl.multiple_of(b * e_block, e_block), e_block)
        return pltpu.make_async_copy(w_hbm.at[:, cols], w_ref.at[b], w_sem.at[b])

    barrier = pltpu.get_barrier_semaphore()
    for d in range(1, n_ctx):
        pl.semaphore_signal(
            barrier, inc=1, device_id={"ctx": lax.rem(i + d, n_ctx)}, device_id_type=MESH
        )
    pl.semaphore_signal(
        barrier, inc=1, device_id={"tp": z * 2 + 1 - y}, device_id_type=MESH
    )

    @pl.when(z > 0)
    def _():
        pl.semaphore_signal(barrier, inc=1, device_id={"tp": me - 2}, device_id_type=MESH)

    @pl.when(z < n_z - 1)
    def _():
        pl.semaphore_signal(barrier, inc=1, device_id={"tp": me + 2}, device_id_type=MESH)

    inputs = [
        pltpu.make_async_copy(src, dst, in_sem.at[n])
        for n, (src, dst) in enumerate(
            ((k_hbm, k_ref), (v_hbm, v_ref), (q_hbm, q_ref), (og_hbm, og_ref))
        )
    ]
    for copy in inputs:
        copy.start()

    def halo_copy(h):
        rows = pl.ds(h * half, half)
        return pltpu.make_async_remote_copy(
            src_ref=kv_ref.at[rows],
            dst_ref=halo_ref.at[rows],
            send_sem=halo_send.at[h],
            recv_sem=halo_recv.at[h],
            device_id={"ctx": lax.rem(i + 1, n_ctx)},
            device_id_type=MESH,
        )

    inputs[0].wait()
    inputs[1].wait()
    for h in range(2):
        rows = slice(h * half, (h + 1) * half)
        kv_ref[rows] = (
            k_ref[rows].astype(jnp.float32) * v_ref[rows].astype(jnp.float32)
        ).astype(jnp.bfloat16)
        if h == 0:
            pl.semaphore_wait(
                barrier, n_ctx + jnp.where(z > 0, 1, 0) + jnp.where(z < n_z - 1, 1, 0)
            )

        @pl.when(i < n_ctx - 1)
        def _():
            halo_copy(h).start()

    @pl.when(i == 0)
    def _():
        halo_ref[...] = jnp.zeros_like(halo_ref)

    mrf_ref[...] = mr_ref[...].astype(jnp.float32)
    rates = upright(rates_ref[...], tokens)
    weights = upright(res_ref[...], tokens) * jnp.sqrt(2.0 * rates / order)
    own = iota((groups, tokens), 1) // order == iota((groups, tokens), 0) % per
    for src, dst, packed in ((rates, rrow_ref, rpack_ref), (weights, wrow_ref, wpack_ref)):
        wide = jnp.where(own, jnp.concatenate([src] * per, axis=1), 0.0)
        dst[...] = jnp.sum(wide.reshape(blocks, per, tokens), axis=1)
        parts = [src[k * per : (k + 1) * per] for k in range(blocks)]
        if blocks < per:
            parts.append(jnp.zeros((per, (per - blocks) * order), jnp.float32))
        joined = jnp.concatenate(parts, axis=1)
        packed[...] = jnp.broadcast_to(
            joined[:, None, :], (per, chan_group, tokens)
        ).reshape(span, tokens)

    square = (tokens, tokens)
    row_i, col_i = iota(square, 0), iota(square, 1)
    def around(row):
        return pltpu.roll(jnp.broadcast_to(row, square), 0, 1, stride=1, stride_axis=0)

    same = row_i // chan_group == col_i // order

    @pl.loop(0, blocks, unroll=half_blocks)
    def _(k):
        r = rrow_ref[pl.ds(k, 1), :]
        place = row_i.astype(jnp.float32)
        high, low = halves(jnp.exp(-r * (tokens - 1.0 - place)))
        tail_ref[k, :tokens, :] = high
        tail_ref[k, tokens:, :] = low
        high, low = halves(jnp.exp(-r * place))
        coef = jnp.concatenate([high, high, low], axis=1)
        coef_ref[k] = coef
        w_sel = jnp.where(
            iota((per, tokens), 1) // order == iota((per, tokens), 0),
            wrow_ref[pl.ds(k, 1), :],
            0.0,
        )
        w_high, w_low = halves(w_sel)
        group_rows = pl.ds(pl.multiple_of(k * per, per), per)
        w_parts = jnp.concatenate([w_high, w_low, w_high], axis=1)
        taps_ref[group_rows, :] = dot(w_parts, coef, ((1,), (1,)))
        mr = mrf_ref[group_rows, :]
        for g in range(per):
            circ = around(mr[g : g + 1, :])
            med_ref[k * per + g, :tokens, :] = jnp.where(row_i > col_i, circ, 0.0).astype(
                jnp.bfloat16
            )
            med_ref[k * per + g, tokens:, :] = jnp.where(row_i <= col_i, circ, 0.0).astype(
                jnp.bfloat16
            )

    def st_copy(d, h):
        return pltpu.make_async_remote_copy(
            src_ref=pack_ref.at[h],
            dst_ref=slot_ref.at[d, h],
            send_sem=st_send.at[d, h],
            recv_sem=st_recv.at[d, h],
            device_id={"ctx": lax.rem(i + d + 1, n_ctx)},
            device_id_type=MESH,
        )

    @pl.loop(0, n_ctx - 1)
    def _(d):
        @pl.when(i < d + 1)
        def _():
            slot_ref[d] = jnp.zeros((2,) + square, jnp.bfloat16)

    @pl.loop(0, blocks, unroll=half_blocks)
    def _(k):
        for g in range(per):
            rows = pl.ds(pl.multiple_of((k * per + g) * chan_group, chan_group), chan_group)
            loc_ref[rows, :] = dot(kv_ref[rows, :], med_ref[k * per + g, tokens:, :])

    @pl.loop(0, n_z)
    def _(p):
        w_copy(target(p) * 2 + 1 - y).start()
        w_copy(target(p) * 2 + y).start()

    inputs[2].wait()
    for h in range(2):

        @pl.when(i > 0)
        def _():
            halo_copy(h).wait_recv()

        @pl.loop(h * half_blocks, (h + 1) * half_blocks, unroll=half_blocks)
        def _(k):
            for g in range(per):
                rows = pl.ds(pl.multiple_of((k * per + g) * chan_group, chan_group), chan_group)
                medium = loc_ref[rows, :] + dot(halo_ref[rows, :], med_ref[k * per + g, :tokens, :])
                gm_ref[rows, :] = (q_ref[rows, :].astype(jnp.float32) * medium).astype(
                    jnp.bfloat16
                )

        packed = jnp.zeros(square, jnp.float32)
        for k in range(h * half_blocks, (h + 1) * half_blocks):
            signal = gm_ref[k * span : (k + 1) * span, :]
            state = dot(jnp.concatenate([signal, signal], axis=1), tail_ref[k])
            state = jnp.where(same, state, 0.0).astype(jnp.bfloat16)
            spread = jnp.where(col_i == k * order + row_i % order, 1.0, 0.0)
            packed += dot(state, spread.astype(jnp.bfloat16))
        pack_ref[h] = packed.astype(jnp.bfloat16)

        @pl.loop(0, n_ctx - 1)
        def _(d):
            @pl.when(i + d + 1 < n_ctx)
            def _():
                st_copy(d, h).start()

    @pl.loop(0, blocks, unroll=half_blocks)
    def _(k):
        taps = taps_ref[pl.ds(pl.multiple_of(k * per, per), per), :]
        for g in range(per):
            rows = pl.ds(pl.multiple_of((k * per + g) * chan_group, chan_group), chan_group)
            circ = jnp.where(row_i <= col_i, around(taps[g : g + 1, :]), 0.0)
            loc_ref[rows, :] = dot(gm_ref[rows, :], circ.astype(jnp.bfloat16))

    inputs[3].wait()
    wide_row = iota((2 * tokens, tokens), 0) % tokens
    wide_col = iota((2 * tokens, tokens), 1)
    for h in range(2):

        @pl.loop(0, n_ctx - 1)
        def _(d):
            @pl.when(i >= d + 1)
            def _():
                st_copy(d, h).wait_recv()

        def add(d, total):
            fade = jnp.exp(-rpack_ref[...] * (tokens * d + 1).astype(jnp.float32))
            return total + fade * slot_ref[d, h].astype(jnp.float32)

        carried = lax.fori_loop(0, n_ctx - 1, add, jnp.zeros(square, jnp.float32))
        carried = jnp.concatenate(halves(carried * wpack_ref[...]), axis=1)
        for k in range(h * half_blocks, (h + 1) * half_blocks):
            rows = slice(k * span, (k + 1) * span)
            gather = jnp.where(wide_row == k * order + wide_col % order, 1.0, 0.0)
            modes = jnp.where(same, dot(carried, gather.astype(jnp.bfloat16)), 0.0)
            high, low = halves(modes)
            entered = dot(jnp.concatenate([high, low, high], axis=1), coef_ref[k], ((1,), (1,)))
            wide = (loc_ref[rows, :] + entered).astype(jnp.bfloat16)
            gated = og_ref[rows, :].astype(jnp.float32) * wide.astype(jnp.float32)
            gt_ref[:, rows] = gated.T.astype(jnp.bfloat16)

    def y_copy(p, c):
        return pltpu.make_async_remote_copy(
            src_ref=ysend.at[p, c],
            dst_ref=yrecv.at[p, c],
            send_sem=ys_sem.at[p, c],
            recv_sem=yr_sem.at[p, c],
            device_id={"tp": z * 2 + 1 - y},
            device_id_type=MESH,
        )

    def z_copy(p, c):
        zt = target(p)
        back = jnp.where(zt < z, 1, 0)
        return pltpu.make_async_remote_copy(
            src_ref=zsend.at[p, c],
            dst_ref=zrecv.at[back, zt, c],
            send_sem=zs_sem.at[p, c],
            recv_sem=zr_sem.at[back, zt, c],
            device_id={"tp": lax.rem(me + 2 - 4 * back + n_tp, n_tp)},
            device_id_type=MESH,
        )

    def z_wait(way, zt, c):
        pltpu.make_async_remote_copy(
            src_ref=zsend.at[0, c],
            dst_ref=zrecv.at[way, zt, c],
            send_sem=zs_sem.at[0, c],
            recv_sem=zr_sem.at[way, zt, c],
            device_id={"tp": z * 2 + 1 - y},
            device_id_type=MESH,
        ).wait_recv()

    def x_copy(p, c):
        zt = target(p)
        back = jnp.where(zt < z, 1, 0)
        end = jnp.where(zt == 0, 0, 1)
        return pltpu.make_async_remote_copy(
            src_ref=xsend.at[end, c],
            dst_ref=xrecv.at[end, c],
            send_sem=xs_sem.at[end, c],
            recv_sem=xr_sem.at[end, c],
            device_id={"tp": lax.rem(me + 2 - 4 * back + n_tp, n_tp)},
            device_id_type=MESH,
        )

    def x_wait(end, c):
        pltpu.make_async_remote_copy(
            src_ref=xsend.at[end, c],
            dst_ref=xrecv.at[end, c],
            send_sem=xs_sem.at[end, c],
            recv_sem=xr_sem.at[end, c],
            device_id={"tp": z * 2 + 1 - y},
            device_id_type=MESH,
        ).wait_recv()

    def at_end(zt):
        return jnp.logical_or(zt == 0, zt == n_z - 1)

    def send_own(p, c):
        zsend[p, c] = acc[p, c].astype(jnp.bfloat16)
        z_copy(p, c).start()

    def send_other(p, c):
        end = jnp.where(target(p) == 0, 0, 1)
        xsend[end, c] = xacc[end, c].astype(jnp.bfloat16)
        x_copy(p, c).start()

    @pl.loop(0, n_z)
    def _(p):
        zt = target(p)
        end = jnp.where(zt == 0, 0, 1)
        joins = jnp.where(zt < z, z < n_z - 1, z > 0)
        w_copy(zt * 2 + 1 - y).wait()
        w_copy(zt * 2 + y).wait()
        for c in range(chunks):
            cols = slice(c * cw, (c + 1) * cw)
            other = dot(gt_ref[...], w_ref[zt * 2 + 1 - y, :, cols])

            def across():
                ysend[p, c] = other.astype(jnp.bfloat16)
                y_copy(p, c).start()

            if c < first:

                @pl.when(at_end(zt))
                def _():
                    xacc[end, c] = other

                pl.when(jnp.logical_not(at_end(zt)))(across)
            else:
                across()
            acc[p, c] = dot(gt_ref[...], w_ref[zt * 2 + y, :, cols])
            if c < first:

                @pl.when(at_end(zt) & (zt != z) & jnp.logical_not(joins))
                def _():
                    send_own(p, c)
                    send_other(p, c)

    @pl.loop(0, n_z - 1)
    def _(p):
        zt = target(p)
        end = jnp.where(zt == 0, 0, 1)
        back = jnp.where(zt < z, 1, 0)
        joins = jnp.where(zt < z, z < n_z - 1, z > 0)

        @pl.loop(0, chunks)
        def _(c):
            ahead = at_end(zt) & (c < first)

            @pl.when(jnp.logical_not(ahead))
            def _():
                y_copy(p, c).wait_recv()
                acc[p, c] += yrecv[p, c].astype(jnp.float32)

            @pl.when(joins)
            def _():
                z_wait(back, zt, c)
                acc[p, c] += zrecv[back, zt, c].astype(jnp.float32)

            @pl.when(jnp.logical_not(ahead & jnp.logical_not(joins)))
            def _():
                send_own(p, c)

            @pl.when(ahead & joins)
            def _():
                x_wait(end, c)
                xacc[end, c] += xrecv[end, c].astype(jnp.float32)
                send_other(p, c)

    own_end = jnp.where(z == 0, 0, 1)

    @pl.when(at_end(z))
    def _():
        for c in range(first):
            x_wait(own_end, c)
            ysend[n_z - 1, c] = (
                xacc[own_end, c] + xrecv[own_end, c].astype(jnp.float32)
            ).astype(jnp.bfloat16)
            y_copy(n_z - 1, c).start()

    for c in list(range(first, chunks)) + list(range(first)):
        y_copy(n_z - 1, c).wait_recv()
        acc[n_z - 1, c] += yrecv[n_z - 1, c].astype(jnp.float32)

        @pl.when(z > 0)
        def _():
            z_wait(0, z, c)
            acc[n_z - 1, c] += zrecv[0, z, c].astype(jnp.float32)

        @pl.when(z < n_z - 1)
        def _():
            z_wait(1, z, c)
            acc[n_z - 1, c] += zrecv[1, z, c].astype(jnp.float32)

        out_ref[c * cw : (c + 1) * cw, :] = acc[n_z - 1, c].T.astype(jnp.bfloat16)

    @pl.when(i < n_ctx - 1)
    def _():
        for h in range(2):
            halo_copy(h).wait_send()

    @pl.loop(0, n_ctx - 1)
    def _(d):
        @pl.when(i + d + 1 < n_ctx)
        def _():
            for h in range(2):
                st_copy(d, h).wait_send()

    @pl.loop(0, n_z)
    def _(p):
        for c in range(chunks):
            if c < first:

                @pl.when(jnp.logical_not(at_end(target(p)) & (p < n_z - 1)))
                def _():
                    y_copy(p, c).wait_send()

                @pl.when(at_end(target(p)) & (p < n_z - 1))
                def _():
                    x_copy(p, c).wait_send()

            else:
                y_copy(p, c).wait_send()

    @pl.loop(0, n_z - 1)
    def _(p):
        for c in range(chunks):
            z_copy(p, c).wait_send()


def per_device(n_ctx, n_tp, q, k, v, og, mr, rates, res, w):
    channels, tokens = q.shape
    groups, order = rates.shape
    assert tokens == mr.shape[1] and groups * order % (2 * tokens) == 0 and tokens % order == 0 and n_tp % 2 == 0
    blocks = groups * order // tokens
    e_block = w.shape[1] // n_tp
    cw = min(e_block, 256)
    chunks = e_block // cw
    some = max(1, chunks // 4)
    n_z = n_tp // 2
    bf, f32 = jnp.bfloat16, jnp.float32
    dma = pltpu.SemaphoreType.DMA
    anywhere = pl.BlockSpec(memory_space=pl.ANY)
    vmem = pl.BlockSpec(memory_space=pltpu.VMEM)
    return pl.pallas_call(
        functools.partial(kernel, n_ctx, n_tp),
        out_shape=jax.ShapeDtypeStruct((e_block, tokens), bf),
        in_specs=[anywhere] * 4 + [vmem] * 3 + [anywhere],
        out_specs=vmem,
        scratch_shapes=[
            pltpu.VMEM((channels, tokens), bf),
            pltpu.VMEM((channels, tokens), bf),
            pltpu.VMEM((channels, tokens), bf),
            pltpu.VMEM((channels, tokens), bf),
            pltpu.VMEM((n_tp, channels, e_block), bf),
            pltpu.VMEM((channels, tokens), bf),
            pltpu.VMEM((channels, tokens), bf),
            pltpu.VMEM((channels, tokens), bf),
            pltpu.VMEM((tokens, channels), bf),
            pltpu.VMEM((groups, tokens), f32),
            pltpu.VMEM((blocks, tokens), f32),
            pltpu.VMEM((blocks, tokens), f32),
            pltpu.VMEM((tokens, tokens), f32),
            pltpu.VMEM((tokens, tokens), f32),
            pltpu.VMEM((groups, 2 * tokens, tokens), bf),
            pltpu.VMEM((groups, tokens), f32),
            pltpu.VMEM((blocks, 2 * tokens, tokens), bf),
            pltpu.VMEM((blocks, tokens, 3 * tokens), bf),
            pltpu.VMEM((channels, tokens), f32),
            pltpu.VMEM((2, tokens, tokens), bf),
            pltpu.VMEM((n_ctx - 1, 2, tokens, tokens), bf),
            pltpu.VMEM((n_z, chunks, tokens, cw), bf),
            pltpu.VMEM((n_z, chunks, tokens, cw), bf),
            pltpu.VMEM((n_z, chunks, tokens, cw), f32),
            pltpu.VMEM((n_z, chunks, tokens, cw), bf),
            pltpu.VMEM((2, n_z, chunks, tokens, cw), bf),
            pltpu.VMEM((2, some, tokens, cw), bf),
            pltpu.VMEM((2, some, tokens, cw), bf),
            pltpu.VMEM((2, some, tokens, cw), f32),
            dma((4,)),
            dma((n_tp,)),
            dma((2,)),
            dma((2,)),
            dma((n_ctx - 1, 2)),
            dma((n_ctx - 1, 2)),
            dma((n_z, chunks)),
            dma((n_z, chunks)),
            dma((n_z, chunks)),
            dma((2, n_z, chunks)),
            dma((2, some)),
            dma((2, some)),
        ],
        compiler_params=pltpu.CompilerParams(
            collective_id=0, has_side_effects=True, vmem_limit_bytes=56 * 2**20
        ),
        name="conv_project",
    )(q, k, v, og, mr, rates.T, res.T, w)


def solution(mesh):
    placed = (
        P("tp", "ctx"),
        P("tp", "ctx"),
        P("tp", "ctx"),
        P("tp", "ctx"),
        P("tp", None),
        P("tp", None),
        P("tp", None),
        P("tp", None),
    )
    return jax.shard_map(
        functools.partial(per_device, mesh.shape["ctx"], mesh.shape["tp"]),
        mesh=mesh,
        in_specs=placed,
        out_specs=P("tp", "ctx"),
        check_vma=False,
    )
```

```python
import functools

import jax
import jax.numpy as jnp
from jax import lax
from jax.experimental import pallas as pl
from jax.experimental.pallas import tpu as pltpu
from jax.sharding import PartitionSpec as P

chan_group = 16
MESH = pl.DeviceIdType.MESH


def dot(a, b, dims=((1,), (0,))):
    return lax.dot_general(a, b, (dims, ((), ())), preferred_element_type=jnp.float32)


def upright(a, size):
    rows, cols = a.shape
    a = jnp.concatenate([a, jnp.zeros((size - rows, cols), a.dtype)], axis=0)
    a = jnp.concatenate([a, jnp.zeros((size, size - cols), a.dtype)], axis=1)
    return a.T[:cols, :rows]


def halves(a):
    high = a.astype(jnp.bfloat16)
    return high, (a - high.astype(jnp.float32)).astype(jnp.bfloat16)


def iota(shape, dim):
    return lax.broadcasted_iota(jnp.int32, shape, dim)


def kernel(
    n_ctx,
    n_tp,
    q_hbm,
    k_hbm,
    v_hbm,
    og_hbm,
    mr_ref,
    rates_ref,
    res_ref,
    w_hbm,
    out_ref,
    q_ref,
    k_ref,
    v_ref,
    og_ref,
    w_ref,
    kv_ref,
    halo_ref,
    gm_ref,
    gt_ref,
    mrf_ref,
    rrow_ref,
    wrow_ref,
    rpack_ref,
    wpack_ref,
    med_ref,
    taps_ref,
    tail_ref,
    coef_ref,
    loc_ref,
    pack_ref,
    slot_ref,
    ysend,
    yrecv,
    acc,
    zsend,
    zrecv,
    xsend,
    xrecv,
    xacc,
    in_sem,
    w_sem,
    halo_send,
    halo_recv,
    st_send,
    st_recv,
    ys_sem,
    yr_sem,
    zs_sem,
    zr_sem,
    xs_sem,
    xr_sem,
):
    channels, tokens = q_hbm.shape
    order = rates_ref.shape[0]
    groups = mr_ref.shape[0]
    per = tokens // order
    blocks = groups // per
    span = per * chan_group
    e_block = out_ref.shape[0]
    cw = ysend.shape[3]
    chunks = e_block // cw
    pair = 2 if chunks % 2 == 0 else 1
    first = chunks // 4
    half = channels // 2
    half_blocks = blocks // 2
    n_z = n_tp // 2
    i = lax.axis_index("ctx")
    me = lax.axis_index("tp")
    z = me // 2
    y = me % 2

    def target(p):
        t = jnp.where(z < n_z // 2, z, n_z - 1 - z)
        j = p + jnp.where(p >= jnp.where(t == 0, 1, n_z - t), 1, 0)
        s = jnp.where(j == 0, n_z - 1, jnp.where(j == 1, 0, n_z - j))
        s = jnp.where(p == n_z - 1, t, s)
        return jnp.where(z < n_z // 2, s, n_z - 1 - s)

    def w_copy(b):
        cols = pl.ds(pl.multiple_of(b * e_block, e_block), e_block)
        return pltpu.make_async_copy(w_hbm.at[:, cols], w_ref.at[b], w_sem.at[b])

    barrier = pltpu.get_barrier_semaphore()
    for d in range(1, n_ctx):
        pl.semaphore_signal(
            barrier, inc=1, device_id={"ctx": lax.rem(i + d, n_ctx)}, device_id_type=MESH
        )
    pl.semaphore_signal(
        barrier, inc=1, device_id={"tp": z * 2 + 1 - y}, device_id_type=MESH
    )

    @pl.when(z > 0)
    def _():
        pl.semaphore_signal(barrier, inc=1, device_id={"tp": me - 2}, device_id_type=MESH)

    @pl.when(z < n_z - 1)
    def _():
        pl.semaphore_signal(barrier, inc=1, device_id={"tp": me + 2}, device_id_type=MESH)

    inputs = [
        pltpu.make_async_copy(src, dst, in_sem.at[n])
        for n, (src, dst) in enumerate(
            ((k_hbm, k_ref), (v_hbm, v_ref), (q_hbm, q_ref), (og_hbm, og_ref))
        )
    ]
    for copy in inputs:
        copy.start()

    def halo_copy(h):
        rows = pl.ds(h * half, half)
        return pltpu.make_async_remote_copy(
            src_ref=kv_ref.at[rows],
            dst_ref=halo_ref.at[rows],
            send_sem=halo_send.at[h],
            recv_sem=halo_recv.at[h],
            device_id={"ctx": lax.rem(i + 1, n_ctx)},
            device_id_type=MESH,
        )

    inputs[0].wait()
    inputs[1].wait()
    for h in range(2):
        rows = slice(h * half, (h + 1) * half)
        kv_ref[rows] = (
            k_ref[rows].astype(jnp.float32) * v_ref[rows].astype(jnp.float32)
        ).astype(jnp.bfloat16)
        if h == 0:
            pl.semaphore_wait(
                barrier, n_ctx + jnp.where(z > 0, 1, 0) + jnp.where(z < n_z - 1, 1, 0)
            )

        @pl.when(i < n_ctx - 1)
        def _():
            halo_copy(h).start()

    @pl.loop(0, n_z)
    def _(p):
        w_copy(target(p) * 2 + 1 - y).start()

    @pl.loop(0, n_z)
    def _(p):
        w_copy(target(p) * 2 + y).start()

    @pl.when(i == 0)
    def _():
        halo_ref[...] = jnp.zeros_like(halo_ref)

    mrf_ref[...] = mr_ref[...].astype(jnp.float32)
    rates = upright(rates_ref[...], tokens)
    weights = upright(res_ref[...], tokens) * jnp.sqrt(2.0 * rates / order)
    own = iota((groups, tokens), 1) // order == iota((groups, tokens), 0) % per
    for src, dst, packed in ((rates, rrow_ref, rpack_ref), (weights, wrow_ref, wpack_ref)):
        wide = jnp.where(own, jnp.concatenate([src] * per, axis=1), 0.0)
        dst[...] = jnp.sum(wide.reshape(blocks, per, tokens), axis=1)
        parts = [src[k * per : (k + 1) * per] for k in range(blocks)]
        if blocks < per:
            parts.append(jnp.zeros((per, (per - blocks) * order), jnp.float32))
        joined = jnp.concatenate(parts, axis=1)
        packed[...] = jnp.broadcast_to(
            joined[:, None, :], (per, chan_group, tokens)
        ).reshape(span, tokens)

    square = (tokens, tokens)
    row_i, col_i = iota(square, 0), iota(square, 1)
    def around(row):
        return pltpu.roll(jnp.broadcast_to(row, square), 0, 1, stride=1, stride_axis=0)

    same = row_i // chan_group == col_i // order

    @pl.loop(0, blocks, unroll=half_blocks)
    def _(k):
        r = rrow_ref[pl.ds(k, 1), :]
        place = row_i.astype(jnp.float32)
        high, low = halves(jnp.exp(-r * (tokens - 1.0 - place)))
        tail_ref[k, :tokens, :] = high
        tail_ref[k, tokens:, :] = low
        high, low = halves(jnp.exp(-r * place))
        coef = jnp.concatenate([high, high, low], axis=1)
        coef_ref[k] = coef
        w_sel = jnp.where(
            iota((per, tokens), 1) // order == iota((per, tokens), 0),
            wrow_ref[pl.ds(k, 1), :],
            0.0,
        )
        w_high, w_low = halves(w_sel)
        group_rows = pl.ds(pl.multiple_of(k * per, per), per)
        w_parts = jnp.concatenate([w_high, w_low, w_high], axis=1)
        taps_ref[group_rows, :] = dot(w_parts, coef, ((1,), (1,)))
        mr = mrf_ref[group_rows, :]
        for g in range(per):
            circ = around(mr[g : g + 1, :])
            med_ref[k * per + g, :tokens, :] = jnp.where(row_i > col_i, circ, 0.0).astype(
                jnp.bfloat16
            )
            med_ref[k * per + g, tokens:, :] = jnp.where(row_i <= col_i, circ, 0.0).astype(
                jnp.bfloat16
            )

    def st_copy(d, h):
        return pltpu.make_async_remote_copy(
            src_ref=pack_ref.at[h],
            dst_ref=slot_ref.at[d, h],
            send_sem=st_send.at[d, h],
            recv_sem=st_recv.at[d, h],
            device_id={"ctx": lax.rem(i + d + 1, n_ctx)},
            device_id_type=MESH,
        )

    @pl.loop(0, n_ctx - 1)
    def _(d):
        @pl.when(i < d + 1)
        def _():
            slot_ref[d] = jnp.zeros((2,) + square, jnp.bfloat16)

    inputs[2].wait()
    for h in range(2):

        @pl.when(i > 0)
        def _():
            halo_copy(h).wait_recv()

        @pl.loop(h * half_blocks, (h + 1) * half_blocks, unroll=half_blocks)
        def _(k):
            for g in range(per):
                rows = pl.ds(pl.multiple_of((k * per + g) * chan_group, chan_group), chan_group)
                signal = jnp.concatenate([halo_ref[rows, :], kv_ref[rows, :]], axis=1)
                medium = dot(signal, med_ref[k * per + g])
                gm_ref[rows, :] = (q_ref[rows, :].astype(jnp.float32) * medium).astype(
                    jnp.bfloat16
                )

        packed = jnp.zeros(square, jnp.float32)
        for k in range(h * half_blocks, (h + 1) * half_blocks):
            signal = gm_ref[k * span : (k + 1) * span, :]
            state = dot(jnp.concatenate([signal, signal], axis=1), tail_ref[k])
            state = jnp.where(same, state, 0.0).astype(jnp.bfloat16)
            spread = jnp.where(col_i == k * order + row_i % order, 1.0, 0.0)
            packed += dot(state, spread.astype(jnp.bfloat16))
        pack_ref[h] = packed.astype(jnp.bfloat16)

        @pl.loop(0, n_ctx - 1)
        def _(d):
            @pl.when(i + d + 1 < n_ctx)
            def _():
                st_copy(d, h).start()

    @pl.loop(0, blocks, unroll=half_blocks)
    def _(k):
        taps = taps_ref[pl.ds(pl.multiple_of(k * per, per), per), :]
        for g in range(per):
            rows = pl.ds(pl.multiple_of((k * per + g) * chan_group, chan_group), chan_group)
            circ = jnp.where(row_i <= col_i, around(taps[g : g + 1, :]), 0.0)
            loc_ref[rows, :] = dot(gm_ref[rows, :], circ.astype(jnp.bfloat16))

    inputs[3].wait()
    wide_row = iota((2 * tokens, tokens), 0) % tokens
    wide_col = iota((2 * tokens, tokens), 1)
    for h in range(2):

        @pl.loop(0, n_ctx - 1)
        def _(d):
            @pl.when(i >= d + 1)
            def _():
                st_copy(d, h).wait_recv()

        def add(d, total):
            fade = jnp.exp(-rpack_ref[...] * (tokens * d + 1).astype(jnp.float32))
            return total + fade * slot_ref[d, h].astype(jnp.float32)

        carried = lax.fori_loop(0, n_ctx - 1, add, jnp.zeros(square, jnp.float32))
        carried = jnp.concatenate(halves(carried * wpack_ref[...]), axis=1)
        for k in range(h * half_blocks, (h + 1) * half_blocks):
            rows = slice(k * span, (k + 1) * span)
            gather = jnp.where(wide_row == k * order + wide_col % order, 1.0, 0.0)
            modes = jnp.where(same, dot(carried, gather.astype(jnp.bfloat16)), 0.0)
            high, low = halves(modes)
            entered = dot(jnp.concatenate([high, low, high], axis=1), coef_ref[k], ((1,), (1,)))
            wide = (loc_ref[rows, :] + entered).astype(jnp.bfloat16)
            gated = og_ref[rows, :].astype(jnp.float32) * wide.astype(jnp.float32)
            gt_ref[:, rows] = gated.T.astype(jnp.bfloat16)

    def y_copy(p, c):
        return pltpu.make_async_remote_copy(
            src_ref=ysend.at[p, c],
            dst_ref=yrecv.at[p, c],
            send_sem=ys_sem.at[p, c],
            recv_sem=yr_sem.at[p, c],
            device_id={"tp": z * 2 + 1 - y},
            device_id_type=MESH,
        )

    def z_copy(p, c):
        zt = target(p)
        back = jnp.where(zt < z, 1, 0)
        return pltpu.make_async_remote_copy(
            src_ref=zsend.at[p, c],
            dst_ref=zrecv.at[back, zt, c],
            send_sem=zs_sem.at[p, c],
            recv_sem=zr_sem.at[back, zt, c],
            device_id={"tp": lax.rem(me + 2 - 4 * back + n_tp, n_tp)},
            device_id_type=MESH,
        )

    def z_wait(way, zt, c):
        pltpu.make_async_remote_copy(
            src_ref=zsend.at[0, c],
            dst_ref=zrecv.at[way, zt, c],
            send_sem=zs_sem.at[0, c],
            recv_sem=zr_sem.at[way, zt, c],
            device_id={"tp": z * 2 + 1 - y},
            device_id_type=MESH,
        ).wait_recv()

    def x_copy(p, c):
        zt = target(p)
        back = jnp.where(zt < z, 1, 0)
        end = jnp.where(zt == 0, 0, 1)
        return pltpu.make_async_remote_copy(
            src_ref=xsend.at[end, c],
            dst_ref=xrecv.at[end, c],
            send_sem=xs_sem.at[end, c],
            recv_sem=xr_sem.at[end, c],
            device_id={"tp": lax.rem(me + 2 - 4 * back + n_tp, n_tp)},
            device_id_type=MESH,
        )

    def x_wait(end, c):
        pltpu.make_async_remote_copy(
            src_ref=xsend.at[end, c],
            dst_ref=xrecv.at[end, c],
            send_sem=xs_sem.at[end, c],
            recv_sem=xr_sem.at[end, c],
            device_id={"tp": z * 2 + 1 - y},
            device_id_type=MESH,
        ).wait_recv()

    def at_end(zt):
        return jnp.logical_or(zt == 0, zt == n_z - 1)

    def send_own(p, c):
        zsend[p, c] = acc[p, c].astype(jnp.bfloat16)
        z_copy(p, c).start()

    def send_other(p, c):
        end = jnp.where(target(p) == 0, 0, 1)
        xsend[end, c] = xacc[end, c].astype(jnp.bfloat16)
        x_copy(p, c).start()

    @pl.loop(0, n_z)
    def _(p):
        zt = target(p)
        end = jnp.where(zt == 0, 0, 1)
        joins = jnp.where(zt < z, z < n_z - 1, z > 0)
        w_copy(zt * 2 + 1 - y).wait()
        w_copy(zt * 2 + y).wait()
        for c in range(chunks):
            if c % pair == 0:
                cols = slice(c * cw, (c + pair) * cw)
                both = dot(gt_ref[...], w_ref[zt * 2 + 1 - y, :, cols])
                mine = dot(gt_ref[...], w_ref[zt * 2 + y, :, cols])
            part = slice(c % pair * cw, (c % pair + 1) * cw)
            other = both[:, part]

            def across():
                ysend[p, c] = other.astype(jnp.bfloat16)
                y_copy(p, c).start()

            if c < first:

                @pl.when(at_end(zt))
                def _():
                    xacc[end, c] = other

                pl.when(jnp.logical_not(at_end(zt)))(across)
            else:
                across()
            acc[p, c] = mine[:, part]
            if c < first:

                @pl.when(at_end(zt) & (zt != z) & jnp.logical_not(joins))
                def _():
                    send_own(p, c)
                    send_other(p, c)

    @pl.loop(0, n_z - 1)
    def _(p):
        zt = target(p)
        end = jnp.where(zt == 0, 0, 1)
        back = jnp.where(zt < z, 1, 0)
        joins = jnp.where(zt < z, z < n_z - 1, z > 0)

        @pl.loop(0, chunks)
        def _(c):
            ahead = at_end(zt) & (c < first)

            @pl.when(jnp.logical_not(ahead))
            def _():
                y_copy(p, c).wait_recv()
                acc[p, c] += yrecv[p, c].astype(jnp.float32)

            @pl.when(joins)
            def _():
                z_wait(back, zt, c)
                acc[p, c] += zrecv[back, zt, c].astype(jnp.float32)

            @pl.when(jnp.logical_not(ahead & jnp.logical_not(joins)))
            def _():
                send_own(p, c)

            @pl.when(ahead & joins)
            def _():
                x_wait(end, c)
                xacc[end, c] += xrecv[end, c].astype(jnp.float32)
                send_other(p, c)

    own_end = jnp.where(z == 0, 0, 1)

    @pl.when(at_end(z))
    def _():
        for c in range(first):
            x_wait(own_end, c)
            ysend[n_z - 1, c] = (
                xacc[own_end, c] + xrecv[own_end, c].astype(jnp.float32)
            ).astype(jnp.bfloat16)
            y_copy(n_z - 1, c).start()

    for c in list(range(first, chunks)) + list(range(first)):
        y_copy(n_z - 1, c).wait_recv()
        acc[n_z - 1, c] += yrecv[n_z - 1, c].astype(jnp.float32)

        @pl.when(z > 0)
        def _():
            z_wait(0, z, c)
            acc[n_z - 1, c] += zrecv[0, z, c].astype(jnp.float32)

        @pl.when(z < n_z - 1)
        def _():
            z_wait(1, z, c)
            acc[n_z - 1, c] += zrecv[1, z, c].astype(jnp.float32)

        out_ref[c * cw : (c + 1) * cw, :] = acc[n_z - 1, c].T.astype(jnp.bfloat16)

    @pl.when(i < n_ctx - 1)
    def _():
        for h in range(2):
            halo_copy(h).wait_send()

    @pl.loop(0, n_ctx - 1)
    def _(d):
        @pl.when(i + d + 1 < n_ctx)
        def _():
            for h in range(2):
                st_copy(d, h).wait_send()

    @pl.loop(0, n_z)
    def _(p):
        for c in range(chunks):
            if c < first:

                @pl.when(jnp.logical_not(at_end(target(p)) & (p < n_z - 1)))
                def _():
                    y_copy(p, c).wait_send()

                @pl.when(at_end(target(p)) & (p < n_z - 1))
                def _():
                    x_copy(p, c).wait_send()

            else:
                y_copy(p, c).wait_send()

    @pl.loop(0, n_z - 1)
    def _(p):
        for c in range(chunks):
            z_copy(p, c).wait_send()


def per_device(n_ctx, n_tp, q, k, v, og, mr, rates, res, w):
    channels, tokens = q.shape
    groups, order = rates.shape
    assert tokens == mr.shape[1] and groups * order % (2 * tokens) == 0 and tokens % order == 0 and n_tp % 2 == 0
    blocks = groups * order // tokens
    e_block = w.shape[1] // n_tp
    cw = min(e_block, 128)
    chunks = e_block // cw
    some = max(1, chunks // 4)
    n_z = n_tp // 2
    bf, f32 = jnp.bfloat16, jnp.float32
    dma = pltpu.SemaphoreType.DMA
    anywhere = pl.BlockSpec(memory_space=pl.ANY)
    vmem = pl.BlockSpec(memory_space=pltpu.VMEM)
    return pl.pallas_call(
        functools.partial(kernel, n_ctx, n_tp),
        out_shape=jax.ShapeDtypeStruct((e_block, tokens), bf),
        in_specs=[anywhere] * 4 + [vmem] * 3 + [anywhere],
        out_specs=vmem,
        scratch_shapes=[
            pltpu.VMEM((channels, tokens), bf),
            pltpu.VMEM((channels, tokens), bf),
            pltpu.VMEM((channels, tokens), bf),
            pltpu.VMEM((channels, tokens), bf),
            pltpu.VMEM((n_tp, channels, e_block), bf),
            pltpu.VMEM((channels, tokens), bf),
            pltpu.VMEM((channels, tokens), bf),
            pltpu.VMEM((channels, tokens), bf),
            pltpu.VMEM((tokens, channels), bf),
            pltpu.VMEM((groups, tokens), f32),
            pltpu.VMEM((blocks, tokens), f32),
            pltpu.VMEM((blocks, tokens), f32),
            pltpu.VMEM((tokens, tokens), f32),
            pltpu.VMEM((tokens, tokens), f32),
            pltpu.VMEM((groups, 2 * tokens, tokens), bf),
            pltpu.VMEM((groups, tokens), f32),
            pltpu.VMEM((blocks, 2 * tokens, tokens), bf),
            pltpu.VMEM((blocks, tokens, 3 * tokens), bf),
            pltpu.VMEM((channels, tokens), f32),
            pltpu.VMEM((2, tokens, tokens), bf),
            pltpu.VMEM((n_ctx - 1, 2, tokens, tokens), bf),
            pltpu.VMEM((n_z, chunks, tokens, cw), bf),
            pltpu.VMEM((n_z, chunks, tokens, cw), bf),
            pltpu.VMEM((n_z, chunks, tokens, cw), f32),
            pltpu.VMEM((n_z, chunks, tokens, cw), bf),
            pltpu.VMEM((2, n_z, chunks, tokens, cw), bf),
            pltpu.VMEM((2, some, tokens, cw), bf),
            pltpu.VMEM((2, some, tokens, cw), bf),
            pltpu.VMEM((2, some, tokens, cw), f32),
            dma((4,)),
            dma((n_tp,)),
            dma((2,)),
            dma((2,)),
            dma((n_ctx - 1, 2)),
            dma((n_ctx - 1, 2)),
            dma((n_z, chunks)),
            dma((n_z, chunks)),
            dma((n_z, chunks)),
            dma((2, n_z, chunks)),
            dma((2, some)),
            dma((2, some)),
        ],
        compiler_params=pltpu.CompilerParams(
            collective_id=0, has_side_effects=True, vmem_limit_bytes=56 * 2**20
        ),
        name="conv_project",
    )(q, k, v, og, mr, rates.T, res.T, w)


def solution(mesh):
    placed = (
        P("tp", "ctx"),
        P("tp", "ctx"),
        P("tp", "ctx"),
        P("tp", "ctx"),
        P("tp", None),
        P("tp", None),
        P("tp", None),
        P("tp", None),
    )
    return jax.shard_map(
        functools.partial(per_device, mesh.shape["ctx"], mesh.shape["tp"]),
        mesh=mesh,
        in_specs=placed,
        out_specs=P("tp", "ctx"),
        check_vma=False,
    )
```

```python
import functools

import jax
import jax.numpy as jnp
from jax import lax
from jax.experimental import pallas as pl
from jax.experimental.pallas import tpu as pltpu
from jax.sharding import PartitionSpec as P

chan_group = 16
MESH = pl.DeviceIdType.MESH


def dot(a, b, dims=((1,), (0,))):
    return lax.dot_general(a, b, (dims, ((), ())), preferred_element_type=jnp.float32)


def upright(a, size):
    rows, cols = a.shape
    a = jnp.concatenate([a, jnp.zeros((size - rows, cols), a.dtype)], axis=0)
    a = jnp.concatenate([a, jnp.zeros((size, size - cols), a.dtype)], axis=1)
    return a.T[:cols, :rows]


def halves(a):
    high = a.astype(jnp.bfloat16)
    return high, (a - high.astype(jnp.float32)).astype(jnp.bfloat16)


def iota(shape, dim):
    return lax.broadcasted_iota(jnp.int32, shape, dim)


def kernel(
    n_ctx,
    n_tp,
    q_hbm,
    k_hbm,
    v_hbm,
    og_hbm,
    mr_ref,
    rates_ref,
    res_ref,
    w_hbm,
    out_ref,
    q_ref,
    k_ref,
    v_ref,
    og_ref,
    w_ref,
    kv_ref,
    halo_ref,
    gm_ref,
    gt_ref,
    mrf_ref,
    rrow_ref,
    wrow_ref,
    rpack_ref,
    wpack_ref,
    med_ref,
    taps_ref,
    tail_ref,
    coef_ref,
    loc_ref,
    pack_ref,
    slot_ref,
    ysend,
    yrecv,
    acc,
    zsend,
    zrecv,
    xsend,
    xrecv,
    xacc,
    in_sem,
    w_sem,
    halo_send,
    halo_recv,
    st_send,
    st_recv,
    ys_sem,
    yr_sem,
    zs_sem,
    zr_sem,
    xs_sem,
    xr_sem,
):
    channels, tokens = q_hbm.shape
    order = rates_ref.shape[0]
    groups = mr_ref.shape[0]
    per = tokens // order
    blocks = groups // per
    span = per * chan_group
    e_block = out_ref.shape[0]
    cw = ysend.shape[3]
    chunks = e_block // cw
    pair = 2 if chunks % 2 == 0 else 1
    first = 3 * chunks // 8
    half = channels // 2
    half_blocks = blocks // 2
    n_z = n_tp // 2
    i = lax.axis_index("ctx")
    me = lax.axis_index("tp")
    z = me // 2
    y = me % 2

    def target(p):
        t = jnp.where(z < n_z // 2, z, n_z - 1 - z)
        j = p + jnp.where(p >= jnp.where(t == 0, 1, n_z - t), 1, 0)
        s = jnp.where(j == 0, n_z - 1, jnp.where(j == 1, 0, n_z - j))
        s = jnp.where(p == n_z - 1, t, s)
        return jnp.where(z < n_z // 2, s, n_z - 1 - s)

    def w_copy(b):
        cols = pl.ds(pl.multiple_of(b * e_block, e_block), e_block)
        return pltpu.make_async_copy(w_hbm.at[:, cols], w_ref.at[b], w_sem.at[b])

    barrier = pltpu.get_barrier_semaphore()
    for d in range(1, n_ctx):
        pl.semaphore_signal(
            barrier, inc=1, device_id={"ctx": lax.rem(i + d, n_ctx)}, device_id_type=MESH
        )
    pl.semaphore_signal(
        barrier, inc=1, device_id={"tp": z * 2 + 1 - y}, device_id_type=MESH
    )

    @pl.when(z > 0)
    def _():
        pl.semaphore_signal(barrier, inc=1, device_id={"tp": me - 2}, device_id_type=MESH)

    @pl.when(z < n_z - 1)
    def _():
        pl.semaphore_signal(barrier, inc=1, device_id={"tp": me + 2}, device_id_type=MESH)

    inputs = [
        pltpu.make_async_copy(src, dst, in_sem.at[n])
        for n, (src, dst) in enumerate(
            ((k_hbm, k_ref), (v_hbm, v_ref), (q_hbm, q_ref), (og_hbm, og_ref))
        )
    ]
    for copy in inputs:
        copy.start()

    def halo_copy(h):
        rows = pl.ds(h * half, half)
        return pltpu.make_async_remote_copy(
            src_ref=kv_ref.at[rows],
            dst_ref=halo_ref.at[rows],
            send_sem=halo_send.at[h],
            recv_sem=halo_recv.at[h],
            device_id={"ctx": lax.rem(i + 1, n_ctx)},
            device_id_type=MESH,
        )

    inputs[0].wait()
    inputs[1].wait()
    for h in range(2):
        rows = slice(h * half, (h + 1) * half)
        kv_ref[rows] = (
            k_ref[rows].astype(jnp.float32) * v_ref[rows].astype(jnp.float32)
        ).astype(jnp.bfloat16)
        if h == 0:
            pl.semaphore_wait(
                barrier, n_ctx + jnp.where(z > 0, 1, 0) + jnp.where(z < n_z - 1, 1, 0)
            )

        @pl.when(i < n_ctx - 1)
        def _():
            halo_copy(h).start()

    @pl.loop(0, n_z)
    def _(p):
        w_copy(target(p) * 2 + 1 - y).start()

    @pl.loop(0, n_z)
    def _(p):
        w_copy(target(p) * 2 + y).start()

    @pl.when(i == 0)
    def _():
        halo_ref[...] = jnp.zeros_like(halo_ref)

    mrf_ref[...] = mr_ref[...].astype(jnp.float32)
    rates = upright(rates_ref[...], tokens)
    weights = upright(res_ref[...], tokens) * jnp.sqrt(2.0 * rates / order)
    own = iota((groups, tokens), 1) // order == iota((groups, tokens), 0) % per
    for src, dst, packed in ((rates, rrow_ref, rpack_ref), (weights, wrow_ref, wpack_ref)):
        wide = jnp.where(own, jnp.concatenate([src] * per, axis=1), 0.0)
        dst[...] = jnp.sum(wide.reshape(blocks, per, tokens), axis=1)
        parts = [src[k * per : (k + 1) * per] for k in range(blocks)]
        if blocks < per:
            parts.append(jnp.zeros((per, (per - blocks) * order), jnp.float32))
        joined = jnp.concatenate(parts, axis=1)
        packed[...] = jnp.broadcast_to(
            joined[:, None, :], (per, chan_group, tokens)
        ).reshape(span, tokens)

    square = (tokens, tokens)
    row_i, col_i = iota(square, 0), iota(square, 1)
    def around(row):
        return pltpu.roll(jnp.broadcast_to(row, square), 0, 1, stride=1, stride_axis=0)

    same = row_i // chan_group == col_i // order

    @pl.loop(0, blocks, unroll=half_blocks)
    def _(k):
        r = rrow_ref[pl.ds(k, 1), :]
        place = row_i.astype(jnp.float32)
        high, low = halves(jnp.exp(-r * (tokens - 1.0 - place)))
        tail_ref[k, :tokens, :] = high
        tail_ref[k, tokens:, :] = low
        high, low = halves(jnp.exp(-r * place))
        coef = jnp.concatenate([high, high, low], axis=1)
        coef_ref[k] = coef
        w_sel = jnp.where(
            iota((per, tokens), 1) // order == iota((per, tokens), 0),
            wrow_ref[pl.ds(k, 1), :],
            0.0,
        )
        w_high, w_low = halves(w_sel)
        group_rows = pl.ds(pl.multiple_of(k * per, per), per)
        w_parts = jnp.concatenate([w_high, w_low, w_high], axis=1)
        taps_ref[group_rows, :] = dot(w_parts, coef, ((1,), (1,)))
        mr = mrf_ref[group_rows, :]
        for g in range(per):
            circ = around(mr[g : g + 1, :])
            med_ref[k * per + g, :tokens, :] = jnp.where(row_i > col_i, circ, 0.0).astype(
                jnp.bfloat16
            )
            med_ref[k * per + g, tokens:, :] = jnp.where(row_i <= col_i, circ, 0.0).astype(
                jnp.bfloat16
            )

    def st_copy(d, h):
        return pltpu.make_async_remote_copy(
            src_ref=pack_ref.at[h],
            dst_ref=slot_ref.at[d, h],
            send_sem=st_send.at[d, h],
            recv_sem=st_recv.at[d, h],
            device_id={"ctx": lax.rem(i + d + 1, n_ctx)},
            device_id_type=MESH,
        )

    @pl.loop(0, n_ctx - 1)
    def _(d):
        @pl.when(i < d + 1)
        def _():
            slot_ref[d] = jnp.zeros((2,) + square, jnp.bfloat16)

    inputs[2].wait()
    for h in range(2):

        @pl.when(i > 0)
        def _():
            halo_copy(h).wait_recv()

        @pl.loop(h * half_blocks, (h + 1) * half_blocks, unroll=half_blocks)
        def _(k):
            for g in range(per):
                rows = pl.ds(pl.multiple_of((k * per + g) * chan_group, chan_group), chan_group)
                signal = jnp.concatenate([halo_ref[rows, :], kv_ref[rows, :]], axis=1)
                medium = dot(signal, med_ref[k * per + g])
                gm_ref[rows, :] = (q_ref[rows, :].astype(jnp.float32) * medium).astype(
                    jnp.bfloat16
                )

        packed = jnp.zeros(square, jnp.float32)
        for k in range(h * half_blocks, (h + 1) * half_blocks):
            signal = gm_ref[k * span : (k + 1) * span, :]
            state = dot(jnp.concatenate([signal, signal], axis=1), tail_ref[k])
            state = jnp.where(same, state, 0.0).astype(jnp.bfloat16)
            spread = jnp.where(col_i == k * order + row_i % order, 1.0, 0.0)
            packed += dot(state, spread.astype(jnp.bfloat16))
        pack_ref[h] = packed.astype(jnp.bfloat16)

        @pl.loop(0, n_ctx - 1)
        def _(d):
            @pl.when(i + d + 1 < n_ctx)
            def _():
                st_copy(d, h).start()

    @pl.loop(0, blocks, unroll=half_blocks)
    def _(k):
        taps = taps_ref[pl.ds(pl.multiple_of(k * per, per), per), :]
        for g in range(per):
            rows = pl.ds(pl.multiple_of((k * per + g) * chan_group, chan_group), chan_group)
            circ = jnp.where(row_i <= col_i, around(taps[g : g + 1, :]), 0.0)
            loc_ref[rows, :] = dot(gm_ref[rows, :], circ.astype(jnp.bfloat16))

    inputs[3].wait()
    wide_row = iota((2 * tokens, tokens), 0) % tokens
    wide_col = iota((2 * tokens, tokens), 1)
    for h in range(2):

        @pl.loop(0, n_ctx - 1)
        def _(d):
            @pl.when(i >= d + 1)
            def _():
                st_copy(d, h).wait_recv()

        def add(d, total):
            fade = jnp.exp(-rpack_ref[...] * (tokens * d + 1).astype(jnp.float32))
            return total + fade * slot_ref[d, h].astype(jnp.float32)

        carried = lax.fori_loop(0, n_ctx - 1, add, jnp.zeros(square, jnp.float32))
        carried = jnp.concatenate(halves(carried * wpack_ref[...]), axis=1)
        for k in range(h * half_blocks, (h + 1) * half_blocks):
            rows = slice(k * span, (k + 1) * span)
            gather = jnp.where(wide_row == k * order + wide_col % order, 1.0, 0.0)
            modes = jnp.where(same, dot(carried, gather.astype(jnp.bfloat16)), 0.0)
            high, low = halves(modes)
            entered = dot(jnp.concatenate([high, low, high], axis=1), coef_ref[k], ((1,), (1,)))
            wide = (loc_ref[rows, :] + entered).astype(jnp.bfloat16)
            gated = og_ref[rows, :].astype(jnp.float32) * wide.astype(jnp.float32)
            gt_ref[:, rows] = gated.T.astype(jnp.bfloat16)

    def y_copy(p, c):
        return pltpu.make_async_remote_copy(
            src_ref=ysend.at[p, c],
            dst_ref=yrecv.at[p, c],
            send_sem=ys_sem.at[p, c],
            recv_sem=yr_sem.at[p, c],
            device_id={"tp": z * 2 + 1 - y},
            device_id_type=MESH,
        )

    def z_copy(p, c):
        zt = target(p)
        back = jnp.where(zt < z, 1, 0)
        return pltpu.make_async_remote_copy(
            src_ref=zsend.at[p, c],
            dst_ref=zrecv.at[back, zt, c],
            send_sem=zs_sem.at[p, c],
            recv_sem=zr_sem.at[back, zt, c],
            device_id={"tp": lax.rem(me + 2 - 4 * back + n_tp, n_tp)},
            device_id_type=MESH,
        )

    def z_wait(way, zt, c):
        pltpu.make_async_remote_copy(
            src_ref=zsend.at[0, c],
            dst_ref=zrecv.at[way, zt, c],
            send_sem=zs_sem.at[0, c],
            recv_sem=zr_sem.at[way, zt, c],
            device_id={"tp": z * 2 + 1 - y},
            device_id_type=MESH,
        ).wait_recv()

    def x_copy(p, c):
        zt = target(p)
        back = jnp.where(zt < z, 1, 0)
        end = jnp.where(zt == 0, 0, 1)
        return pltpu.make_async_remote_copy(
            src_ref=xsend.at[end, c],
            dst_ref=xrecv.at[end, c],
            send_sem=xs_sem.at[end, c],
            recv_sem=xr_sem.at[end, c],
            device_id={"tp": lax.rem(me + 2 - 4 * back + n_tp, n_tp)},
            device_id_type=MESH,
        )

    def x_wait(end, c):
        pltpu.make_async_remote_copy(
            src_ref=xsend.at[end, c],
            dst_ref=xrecv.at[end, c],
            send_sem=xs_sem.at[end, c],
            recv_sem=xr_sem.at[end, c],
            device_id={"tp": z * 2 + 1 - y},
            device_id_type=MESH,
        ).wait_recv()

    def at_end(zt):
        return jnp.logical_or(zt == 0, zt == n_z - 1)

    def send_own(p, c):
        zsend[p, c] = acc[p, c].astype(jnp.bfloat16)
        z_copy(p, c).start()

    def send_other(p, c):
        end = jnp.where(target(p) == 0, 0, 1)
        xsend[end, c] = xacc[end, c].astype(jnp.bfloat16)
        x_copy(p, c).start()

    @pl.loop(0, n_z)
    def _(p):
        zt = target(p)
        end = jnp.where(zt == 0, 0, 1)
        joins = jnp.where(zt < z, z < n_z - 1, z > 0)
        w_copy(zt * 2 + 1 - y).wait()
        w_copy(zt * 2 + y).wait()
        for c in range(chunks):
            if c % pair == 0:
                cols = slice(c * cw, (c + pair) * cw)
                both = dot(gt_ref[...], w_ref[zt * 2 + 1 - y, :, cols])
                mine = dot(gt_ref[...], w_ref[zt * 2 + y, :, cols])
            part = slice(c % pair * cw, (c % pair + 1) * cw)
            other = both[:, part]

            def across():
                ysend[p, c] = other.astype(jnp.bfloat16)
                y_copy(p, c).start()

            if c < first:

                @pl.when(at_end(zt))
                def _():
                    xacc[end, c] = other

                pl.when(jnp.logical_not(at_end(zt)))(across)
            else:
                across()
            acc[p, c] = mine[:, part]
            if c < first:

                @pl.when(at_end(zt) & (zt != z) & jnp.logical_not(joins))
                def _():
                    send_own(p, c)
                    send_other(p, c)

    @pl.loop(0, n_z - 1)
    def _(p):
        zt = target(p)
        end = jnp.where(zt == 0, 0, 1)
        back = jnp.where(zt < z, 1, 0)
        joins = jnp.where(zt < z, z < n_z - 1, z > 0)

        @pl.loop(0, chunks)
        def _(c):
            ahead = at_end(zt) & (c < first)

            @pl.when(jnp.logical_not(ahead))
            def _():
                y_copy(p, c).wait_recv()
                acc[p, c] += yrecv[p, c].astype(jnp.float32)

            @pl.when(joins)
            def _():
                z_wait(back, zt, c)
                acc[p, c] += zrecv[back, zt, c].astype(jnp.float32)

            @pl.when(jnp.logical_not(ahead & jnp.logical_not(joins)))
            def _():
                send_own(p, c)

            @pl.when(ahead & joins)
            def _():
                x_wait(end, c)
                xacc[end, c] += xrecv[end, c].astype(jnp.float32)
                send_other(p, c)

    own_end = jnp.where(z == 0, 0, 1)

    @pl.when(at_end(z))
    def _():
        for c in range(first):
            x_wait(own_end, c)
            ysend[n_z - 1, c] = (
                xacc[own_end, c] + xrecv[own_end, c].astype(jnp.float32)
            ).astype(jnp.bfloat16)
            y_copy(n_z - 1, c).start()

    for c in list(range(first, chunks)) + list(range(first)):
        y_copy(n_z - 1, c).wait_recv()
        acc[n_z - 1, c] += yrecv[n_z - 1, c].astype(jnp.float32)

        @pl.when(z > 0)
        def _():
            z_wait(0, z, c)
            acc[n_z - 1, c] += zrecv[0, z, c].astype(jnp.float32)

        @pl.when(z < n_z - 1)
        def _():
            z_wait(1, z, c)
            acc[n_z - 1, c] += zrecv[1, z, c].astype(jnp.float32)

        out_ref[c * cw : (c + 1) * cw, :] = acc[n_z - 1, c].T.astype(jnp.bfloat16)

    @pl.when(i < n_ctx - 1)
    def _():
        for h in range(2):
            halo_copy(h).wait_send()

    @pl.loop(0, n_ctx - 1)
    def _(d):
        @pl.when(i + d + 1 < n_ctx)
        def _():
            for h in range(2):
                st_copy(d, h).wait_send()

    @pl.loop(0, n_z)
    def _(p):
        for c in range(chunks):
            if c < first:

                @pl.when(jnp.logical_not(at_end(target(p)) & (p < n_z - 1)))
                def _():
                    y_copy(p, c).wait_send()

                @pl.when(at_end(target(p)) & (p < n_z - 1))
                def _():
                    x_copy(p, c).wait_send()

            else:
                y_copy(p, c).wait_send()

    @pl.loop(0, n_z - 1)
    def _(p):
        for c in range(chunks):
            z_copy(p, c).wait_send()


def per_device(n_ctx, n_tp, q, k, v, og, mr, rates, res, w):
    channels, tokens = q.shape
    groups, order = rates.shape
    assert tokens == mr.shape[1] and groups * order % (2 * tokens) == 0 and tokens % order == 0 and n_tp % 2 == 0
    blocks = groups * order // tokens
    e_block = w.shape[1] // n_tp
    cw = min(e_block, 128)
    chunks = e_block // cw
    some = max(1, 3 * chunks // 8)
    n_z = n_tp // 2
    bf, f32 = jnp.bfloat16, jnp.float32
    dma = pltpu.SemaphoreType.DMA
    anywhere = pl.BlockSpec(memory_space=pl.ANY)
    vmem = pl.BlockSpec(memory_space=pltpu.VMEM)
    return pl.pallas_call(
        functools.partial(kernel, n_ctx, n_tp),
        out_shape=jax.ShapeDtypeStruct((e_block, tokens), bf),
        in_specs=[anywhere] * 4 + [vmem] * 3 + [anywhere],
        out_specs=vmem,
        scratch_shapes=[
            pltpu.VMEM((channels, tokens), bf),
            pltpu.VMEM((channels, tokens), bf),
            pltpu.VMEM((channels, tokens), bf),
            pltpu.VMEM((channels, tokens), bf),
            pltpu.VMEM((n_tp, channels, e_block), bf),
            pltpu.VMEM((channels, tokens), bf),
            pltpu.VMEM((channels, tokens), bf),
            pltpu.VMEM((channels, tokens), bf),
            pltpu.VMEM((tokens, channels), bf),
            pltpu.VMEM((groups, tokens), f32),
            pltpu.VMEM((blocks, tokens), f32),
            pltpu.VMEM((blocks, tokens), f32),
            pltpu.VMEM((tokens, tokens), f32),
            pltpu.VMEM((tokens, tokens), f32),
            pltpu.VMEM((groups, 2 * tokens, tokens), bf),
            pltpu.VMEM((groups, tokens), f32),
            pltpu.VMEM((blocks, 2 * tokens, tokens), bf),
            pltpu.VMEM((blocks, tokens, 3 * tokens), bf),
            pltpu.VMEM((channels, tokens), f32),
            pltpu.VMEM((2, tokens, tokens), bf),
            pltpu.VMEM((n_ctx - 1, 2, tokens, tokens), bf),
            pltpu.VMEM((n_z, chunks, tokens, cw), bf),
            pltpu.VMEM((n_z, chunks, tokens, cw), bf),
            pltpu.VMEM((n_z, chunks, tokens, cw), f32),
            pltpu.VMEM((n_z, chunks, tokens, cw), bf),
            pltpu.VMEM((2, n_z, chunks, tokens, cw), bf),
            pltpu.VMEM((2, some, tokens, cw), bf),
            pltpu.VMEM((2, some, tokens, cw), bf),
            pltpu.VMEM((2, some, tokens, cw), f32),
            dma((4,)),
            dma((n_tp,)),
            dma((2,)),
            dma((2,)),
            dma((n_ctx - 1, 2)),
            dma((n_ctx - 1, 2)),
            dma((n_z, chunks)),
            dma((n_z, chunks)),
            dma((n_z, chunks)),
            dma((2, n_z, chunks)),
            dma((2, some)),
            dma((2, some)),
        ],
        compiler_params=pltpu.CompilerParams(
            collective_id=0, has_side_effects=True, vmem_limit_bytes=56 * 2**20
        ),
        name="conv_project",
    )(q, k, v, og, mr, rates.T, res.T, w)


def solution(mesh):
    placed = (
        P("tp", "ctx"),
        P("tp", "ctx"),
        P("tp", "ctx"),
        P("tp", "ctx"),
        P("tp", None),
        P("tp", None),
        P("tp", None),
        P("tp", None),
    )
    return jax.shard_map(
        functools.partial(per_device, mesh.shape["ctx"], mesh.shape["tp"]),
        mesh=mesh,
        in_specs=placed,
        out_specs=P("tp", "ctx"),
        check_vma=False,
    )
```

```python
import functools

import jax
import jax.numpy as jnp
from jax import lax
from jax.experimental import pallas as pl
from jax.experimental.pallas import tpu as pltpu
from jax.sharding import PartitionSpec as P

chan_group = 16
MESH = pl.DeviceIdType.MESH


def dot(a, b, dims=((1,), (0,))):
    return lax.dot_general(a, b, (dims, ((), ())), preferred_element_type=jnp.float32)


def upright(a, size):
    rows, cols = a.shape
    a = jnp.concatenate([a, jnp.zeros((size - rows, cols), a.dtype)], axis=0)
    a = jnp.concatenate([a, jnp.zeros((size, size - cols), a.dtype)], axis=1)
    return a.T[:cols, :rows]


def halves(a):
    high = a.astype(jnp.bfloat16)
    return high, (a - high.astype(jnp.float32)).astype(jnp.bfloat16)


def iota(shape, dim):
    return lax.broadcasted_iota(jnp.int32, shape, dim)


def kernel(
    n_ctx,
    n_tp,
    q_hbm,
    k_hbm,
    v_hbm,
    og_hbm,
    mr_ref,
    rates_ref,
    res_ref,
    w_hbm,
    out_ref,
    q_ref,
    k_ref,
    v_ref,
    og_ref,
    w_ref,
    kv_ref,
    halo_ref,
    gm_ref,
    gt_ref,
    mrf_ref,
    rrow_ref,
    wrow_ref,
    rpack_ref,
    wpack_ref,
    med_ref,
    taps_ref,
    tail_ref,
    coef_ref,
    loc_ref,
    pack_ref,
    slot_ref,
    ysend,
    yrecv,
    acc,
    zsend,
    zrecv,
    xsend,
    xrecv,
    xacc,
    in_sem,
    w_sem,
    halo_send,
    halo_recv,
    st_send,
    st_recv,
    ys_sem,
    yr_sem,
    zs_sem,
    zr_sem,
    xs_sem,
    xr_sem,
):
    channels, tokens = q_hbm.shape
    order = rates_ref.shape[0]
    groups = mr_ref.shape[0]
    per = tokens // order
    blocks = groups // per
    span = per * chan_group
    e_block = out_ref.shape[0]
    cw = ysend.shape[3]
    chunks = e_block // cw
    pair = 2 if chunks % 2 == 0 else 1
    first = 3 * chunks // 8
    half = channels // 2
    half_blocks = blocks // 2
    n_z = n_tp // 2
    i = lax.axis_index("ctx")
    me = lax.axis_index("tp")
    z = me // 2
    y = me % 2

    def target(p):
        t = jnp.where(z < n_z // 2, z, n_z - 1 - z)
        j = p + jnp.where(p >= jnp.where(t == 0, 1, n_z - t), 1, 0)
        s = jnp.where(j == 0, n_z - 1, jnp.where(j == 1, 0, n_z - j))
        s = jnp.where(p == n_z - 1, t, s)
        return jnp.where(z < n_z // 2, s, n_z - 1 - s)

    def w_copy(b):
        cols = pl.ds(pl.multiple_of(b * e_block, e_block), e_block)
        return pltpu.make_async_copy(w_hbm.at[:, cols], w_ref.at[b], w_sem.at[b])

    barrier = pltpu.get_barrier_semaphore()
    for d in range(1, n_ctx):
        pl.semaphore_signal(
            barrier, inc=1, device_id={"ctx": lax.rem(i + d, n_ctx)}, device_id_type=MESH
        )
    pl.semaphore_signal(
        barrier, inc=1, device_id={"tp": z * 2 + 1 - y}, device_id_type=MESH
    )

    @pl.when(z > 0)
    def _():
        pl.semaphore_signal(barrier, inc=1, device_id={"tp": me - 2}, device_id_type=MESH)

    @pl.when(z < n_z - 1)
    def _():
        pl.semaphore_signal(barrier, inc=1, device_id={"tp": me + 2}, device_id_type=MESH)

    inputs = [
        pltpu.make_async_copy(src, dst, in_sem.at[n])
        for n, (src, dst) in enumerate(
            ((k_hbm, k_ref), (v_hbm, v_ref), (q_hbm, q_ref), (og_hbm, og_ref))
        )
    ]
    for copy in inputs:
        copy.start()

    def halo_copy(h):
        rows = pl.ds(h * half, half)
        return pltpu.make_async_remote_copy(
            src_ref=kv_ref.at[rows],
            dst_ref=halo_ref.at[rows],
            send_sem=halo_send.at[h],
            recv_sem=halo_recv.at[h],
            device_id={"ctx": lax.rem(i + 1, n_ctx)},
            device_id_type=MESH,
        )

    inputs[0].wait()
    inputs[1].wait()
    for h in range(2):
        rows = slice(h * half, (h + 1) * half)
        kv_ref[rows] = (
            k_ref[rows].astype(jnp.float32) * v_ref[rows].astype(jnp.float32)
        ).astype(jnp.bfloat16)
        if h == 0:
            pl.semaphore_wait(
                barrier, n_ctx + jnp.where(z > 0, 1, 0) + jnp.where(z < n_z - 1, 1, 0)
            )

        @pl.when(i < n_ctx - 1)
        def _():
            halo_copy(h).start()

    @pl.loop(0, n_z)
    def _(p):
        w_copy(target(p) * 2 + 1 - y).start()

    @pl.loop(0, n_z)
    def _(p):
        w_copy(target(p) * 2 + y).start()

    @pl.when(i == 0)
    def _():
        halo_ref[...] = jnp.zeros_like(halo_ref)

    mrf_ref[...] = mr_ref[...].astype(jnp.float32)
    rates = upright(rates_ref[...], tokens)
    weights = upright(res_ref[...], tokens) * jnp.sqrt(2.0 * rates / order)
    own = iota((groups, tokens), 1) // order == iota((groups, tokens), 0) % per
    for src, dst, packed in ((rates, rrow_ref, rpack_ref), (weights, wrow_ref, wpack_ref)):
        wide = jnp.where(own, jnp.concatenate([src] * per, axis=1), 0.0)
        dst[...] = jnp.sum(wide.reshape(blocks, per, tokens), axis=1)
        parts = [src[k * per : (k + 1) * per] for k in range(blocks)]
        if blocks < per:
            parts.append(jnp.zeros((per, (per - blocks) * order), jnp.float32))
        joined = jnp.concatenate(parts, axis=1)
        packed[...] = jnp.broadcast_to(
            joined[:, None, :], (per, chan_group, tokens)
        ).reshape(span, tokens)

    square = (tokens, tokens)
    row_i, col_i = iota(square, 0), iota(square, 1)
    def around(row):
        return pltpu.roll(jnp.broadcast_to(row, square), 0, 1, stride=1, stride_axis=0)

    same = row_i // chan_group == col_i // order

    @pl.loop(0, blocks, unroll=half_blocks)
    def _(k):
        r = rrow_ref[pl.ds(k, 1), :]
        place = row_i.astype(jnp.float32)
        high, low = halves(jnp.exp(-r * (tokens - 1.0 - place)))
        tail_ref[k, :tokens, :] = high
        tail_ref[k, tokens:, :] = low
        high, low = halves(jnp.exp(-r * place))
        coef = jnp.concatenate([high, high, low], axis=1)
        coef_ref[k] = coef
        w_sel = jnp.where(
            iota((per, tokens), 1) // order == iota((per, tokens), 0),
            wrow_ref[pl.ds(k, 1), :],
            0.0,
        )
        w_high, w_low = halves(w_sel)
        group_rows = pl.ds(pl.multiple_of(k * per, per), per)
        w_parts = jnp.concatenate([w_high, w_low, w_high], axis=1)
        taps_ref[group_rows, :] = dot(w_parts, coef, ((1,), (1,)))
        mr = mrf_ref[group_rows, :]
        for g in range(per):
            circ = around(mr[g : g + 1, :])
            med_ref[k * per + g, :tokens, :] = jnp.where(row_i > col_i, circ, 0.0).astype(
                jnp.bfloat16
            )
            med_ref[k * per + g, tokens:, :] = jnp.where(row_i <= col_i, circ, 0.0).astype(
                jnp.bfloat16
            )

    def st_copy(d, h):
        return pltpu.make_async_remote_copy(
            src_ref=pack_ref.at[h],
            dst_ref=slot_ref.at[d, h],
            send_sem=st_send.at[d, h],
            recv_sem=st_recv.at[d, h],
            device_id={"ctx": lax.rem(i + d + 1, n_ctx)},
            device_id_type=MESH,
        )

    @pl.loop(0, n_ctx - 1)
    def _(d):
        @pl.when(i < d + 1)
        def _():
            slot_ref[d] = jnp.zeros((2,) + square, jnp.bfloat16)

    inputs[2].wait()
    for h in range(2):

        @pl.when(i > 0)
        def _():
            halo_copy(h).wait_recv()

        @pl.loop(h * half_blocks, (h + 1) * half_blocks, unroll=half_blocks)
        def _(k):
            for g in range(per):
                rows = pl.ds(pl.multiple_of((k * per + g) * chan_group, chan_group), chan_group)
                signal = jnp.concatenate([halo_ref[rows, :], kv_ref[rows, :]], axis=1)
                medium = dot(signal, med_ref[k * per + g])
                gm_ref[rows, :] = (q_ref[rows, :].astype(jnp.float32) * medium).astype(
                    jnp.bfloat16
                )

        packed = jnp.zeros(square, jnp.float32)
        for k in range(h * half_blocks, (h + 1) * half_blocks):
            signal = gm_ref[k * span : (k + 1) * span, :]
            state = dot(jnp.concatenate([signal, signal], axis=1), tail_ref[k])
            state = jnp.where(same, state, 0.0).astype(jnp.bfloat16)
            spread = jnp.where(col_i == k * order + row_i % order, 1.0, 0.0)
            packed += dot(state, spread.astype(jnp.bfloat16))
        pack_ref[h] = packed.astype(jnp.bfloat16)

        @pl.loop(0, n_ctx - 1)
        def _(d):
            @pl.when(i + d + 1 < n_ctx)
            def _():
                st_copy(d, h).start()

    @pl.loop(0, blocks, unroll=half_blocks)
    def _(k):
        taps = taps_ref[pl.ds(pl.multiple_of(k * per, per), per), :]
        for g in range(per):
            rows = pl.ds(pl.multiple_of((k * per + g) * chan_group, chan_group), chan_group)
            circ = jnp.where(row_i <= col_i, around(taps[g : g + 1, :]), 0.0)
            loc_ref[rows, :] = dot(gm_ref[rows, :], circ.astype(jnp.bfloat16))

    inputs[3].wait()
    wide_row = iota((2 * tokens, tokens), 0) % tokens
    wide_col = iota((2 * tokens, tokens), 1)
    for h in range(2):

        @pl.loop(0, n_ctx - 1)
        def _(d):
            @pl.when(i >= d + 1)
            def _():
                st_copy(d, h).wait_recv()

        def add(d, total):
            fade = jnp.exp(-rpack_ref[...] * (tokens * d + 1).astype(jnp.float32))
            return total + fade * slot_ref[d, h].astype(jnp.float32)

        carried = lax.fori_loop(0, n_ctx - 1, add, jnp.zeros(square, jnp.float32))
        carried = jnp.concatenate(halves(carried * wpack_ref[...]), axis=1)
        for k in range(h * half_blocks, (h + 1) * half_blocks):
            rows = slice(k * span, (k + 1) * span)
            gather = jnp.where(wide_row == k * order + wide_col % order, 1.0, 0.0)
            modes = jnp.where(same, dot(carried, gather.astype(jnp.bfloat16)), 0.0)
            high, low = halves(modes)
            entered = dot(jnp.concatenate([high, low, high], axis=1), coef_ref[k], ((1,), (1,)))
            wide = (loc_ref[rows, :] + entered).astype(jnp.bfloat16)
            gated = og_ref[rows, :].astype(jnp.float32) * wide.astype(jnp.float32)
            gt_ref[:, rows] = gated.astype(jnp.bfloat16).T

    def y_copy(p, c):
        return pltpu.make_async_remote_copy(
            src_ref=ysend.at[p, c],
            dst_ref=yrecv.at[p, c],
            send_sem=ys_sem.at[p, c],
            recv_sem=yr_sem.at[p, c],
            device_id={"tp": z * 2 + 1 - y},
            device_id_type=MESH,
        )

    def z_copy(p, c):
        zt = target(p)
        back = jnp.where(zt < z, 1, 0)
        return pltpu.make_async_remote_copy(
            src_ref=zsend.at[p, c],
            dst_ref=zrecv.at[back, zt, c],
            send_sem=zs_sem.at[p, c],
            recv_sem=zr_sem.at[back, zt, c],
            device_id={"tp": lax.rem(me + 2 - 4 * back + n_tp, n_tp)},
            device_id_type=MESH,
        )

    def z_wait(way, zt, c):
        pltpu.make_async_remote_copy(
            src_ref=zsend.at[0, c],
            dst_ref=zrecv.at[way, zt, c],
            send_sem=zs_sem.at[0, c],
            recv_sem=zr_sem.at[way, zt, c],
            device_id={"tp": z * 2 + 1 - y},
            device_id_type=MESH,
        ).wait_recv()

    def x_copy(p, c):
        zt = target(p)
        back = jnp.where(zt < z, 1, 0)
        end = jnp.where(zt == 0, 0, 1)
        return pltpu.make_async_remote_copy(
            src_ref=xsend.at[end, c],
            dst_ref=xrecv.at[end, c],
            send_sem=xs_sem.at[end, c],
            recv_sem=xr_sem.at[end, c],
            device_id={"tp": lax.rem(me + 2 - 4 * back + n_tp, n_tp)},
            device_id_type=MESH,
        )

    def x_wait(end, c):
        pltpu.make_async_remote_copy(
            src_ref=xsend.at[end, c],
            dst_ref=xrecv.at[end, c],
            send_sem=xs_sem.at[end, c],
            recv_sem=xr_sem.at[end, c],
            device_id={"tp": z * 2 + 1 - y},
            device_id_type=MESH,
        ).wait_recv()

    def at_end(zt):
        return jnp.logical_or(zt == 0, zt == n_z - 1)

    def send_own(p, c):
        zsend[p, c] = acc[p, c].astype(jnp.bfloat16)
        z_copy(p, c).start()

    def send_other(p, c):
        end = jnp.where(target(p) == 0, 0, 1)
        xsend[end, c] = xacc[end, c].astype(jnp.bfloat16)
        x_copy(p, c).start()

    @pl.loop(0, n_z)
    def _(p):
        zt = target(p)
        end = jnp.where(zt == 0, 0, 1)
        joins = jnp.where(zt < z, z < n_z - 1, z > 0)
        w_copy(zt * 2 + 1 - y).wait()
        w_copy(zt * 2 + y).wait()
        for c in range(chunks):
            if c % pair == 0:
                cols = slice(c * cw, (c + pair) * cw)
                both = dot(gt_ref[...], w_ref[zt * 2 + 1 - y, :, cols])
                mine = dot(gt_ref[...], w_ref[zt * 2 + y, :, cols])
            part = slice(c % pair * cw, (c % pair + 1) * cw)
            other = both[:, part]

            def across():
                ysend[p, c] = other.astype(jnp.bfloat16)
                y_copy(p, c).start()

            if c < first:

                @pl.when(at_end(zt))
                def _():
                    xacc[end, c] = other

                pl.when(jnp.logical_not(at_end(zt)))(across)
            else:
                across()
            acc[p, c] = mine[:, part]
            if c < first:

                @pl.when(at_end(zt) & (zt != z) & jnp.logical_not(joins))
                def _():
                    send_own(p, c)
                    send_other(p, c)

    @pl.loop(0, n_z - 1)
    def _(p):
        zt = target(p)
        end = jnp.where(zt == 0, 0, 1)
        back = jnp.where(zt < z, 1, 0)
        joins = jnp.where(zt < z, z < n_z - 1, z > 0)

        @pl.loop(0, chunks)
        def _(c):
            ahead = at_end(zt) & (c < first)

            @pl.when(jnp.logical_not(ahead))
            def _():
                y_copy(p, c).wait_recv()
                acc[p, c] += yrecv[p, c].astype(jnp.float32)

            @pl.when(joins)
            def _():
                z_wait(back, zt, c)
                acc[p, c] += zrecv[back, zt, c].astype(jnp.float32)

            @pl.when(jnp.logical_not(ahead & jnp.logical_not(joins)))
            def _():
                send_own(p, c)

            @pl.when(ahead & joins)
            def _():
                x_wait(end, c)
                xacc[end, c] += xrecv[end, c].astype(jnp.float32)
                send_other(p, c)

    own_end = jnp.where(z == 0, 0, 1)

    @pl.when(at_end(z))
    def _():
        for c in range(first):
            x_wait(own_end, c)
            ysend[n_z - 1, c] = (
                xacc[own_end, c] + xrecv[own_end, c].astype(jnp.float32)
            ).astype(jnp.bfloat16)
            y_copy(n_z - 1, c).start()

    for c in list(range(first, chunks)) + list(range(first)):
        y_copy(n_z - 1, c).wait_recv()
        acc[n_z - 1, c] += yrecv[n_z - 1, c].astype(jnp.float32)

        @pl.when(z > 0)
        def _():
            z_wait(0, z, c)
            acc[n_z - 1, c] += zrecv[0, z, c].astype(jnp.float32)

        @pl.when(z < n_z - 1)
        def _():
            z_wait(1, z, c)
            acc[n_z - 1, c] += zrecv[1, z, c].astype(jnp.float32)

        out_ref[c * cw : (c + 1) * cw, :] = acc[n_z - 1, c].T.astype(jnp.bfloat16)

    @pl.when(i < n_ctx - 1)
    def _():
        for h in range(2):
            halo_copy(h).wait_send()

    @pl.loop(0, n_ctx - 1)
    def _(d):
        @pl.when(i + d + 1 < n_ctx)
        def _():
            for h in range(2):
                st_copy(d, h).wait_send()

    @pl.loop(0, n_z)
    def _(p):
        for c in range(chunks):
            if c < first:

                @pl.when(jnp.logical_not(at_end(target(p)) & (p < n_z - 1)))
                def _():
                    y_copy(p, c).wait_send()

                @pl.when(at_end(target(p)) & (p < n_z - 1))
                def _():
                    x_copy(p, c).wait_send()

            else:
                y_copy(p, c).wait_send()

    @pl.loop(0, n_z - 1)
    def _(p):
        for c in range(chunks):
            z_copy(p, c).wait_send()


def per_device(n_ctx, n_tp, q, k, v, og, mr, rates, res, w):
    channels, tokens = q.shape
    groups, order = rates.shape
    assert tokens == mr.shape[1] and groups * order % (2 * tokens) == 0 and tokens % order == 0 and n_tp % 2 == 0
    blocks = groups * order // tokens
    e_block = w.shape[1] // n_tp
    cw = min(e_block, 128)
    chunks = e_block // cw
    some = max(1, 3 * chunks // 8)
    n_z = n_tp // 2
    bf, f32 = jnp.bfloat16, jnp.float32
    dma = pltpu.SemaphoreType.DMA
    anywhere = pl.BlockSpec(memory_space=pl.ANY)
    vmem = pl.BlockSpec(memory_space=pltpu.VMEM)
    return pl.pallas_call(
        functools.partial(kernel, n_ctx, n_tp),
        out_shape=jax.ShapeDtypeStruct((e_block, tokens), bf),
        in_specs=[anywhere] * 4 + [vmem] * 3 + [anywhere],
        out_specs=vmem,
        scratch_shapes=[
            pltpu.VMEM((channels, tokens), bf),
            pltpu.VMEM((channels, tokens), bf),
            pltpu.VMEM((channels, tokens), bf),
            pltpu.VMEM((channels, tokens), bf),
            pltpu.VMEM((n_tp, channels, e_block), bf),
            pltpu.VMEM((channels, tokens), bf),
            pltpu.VMEM((channels, tokens), bf),
            pltpu.VMEM((channels, tokens), bf),
            pltpu.VMEM((tokens, channels), bf),
            pltpu.VMEM((groups, tokens), f32),
            pltpu.VMEM((blocks, tokens), f32),
            pltpu.VMEM((blocks, tokens), f32),
            pltpu.VMEM((tokens, tokens), f32),
            pltpu.VMEM((tokens, tokens), f32),
            pltpu.VMEM((groups, 2 * tokens, tokens), bf),
            pltpu.VMEM((groups, tokens), f32),
            pltpu.VMEM((blocks, 2 * tokens, tokens), bf),
            pltpu.VMEM((blocks, tokens, 3 * tokens), bf),
            pltpu.VMEM((channels, tokens), f32),
            pltpu.VMEM((2, tokens, tokens), bf),
            pltpu.VMEM((n_ctx - 1, 2, tokens, tokens), bf),
            pltpu.VMEM((n_z, chunks, tokens, cw), bf),
            pltpu.VMEM((n_z, chunks, tokens, cw), bf),
            pltpu.VMEM((n_z, chunks, tokens, cw), f32),
            pltpu.VMEM((n_z, chunks, tokens, cw), bf),
            pltpu.VMEM((2, n_z, chunks, tokens, cw), bf),
            pltpu.VMEM((2, some, tokens, cw), bf),
            pltpu.VMEM((2, some, tokens, cw), bf),
            pltpu.VMEM((2, some, tokens, cw), f32),
            dma((4,)),
            dma((n_tp,)),
            dma((2,)),
            dma((2,)),
            dma((n_ctx - 1, 2)),
            dma((n_ctx - 1, 2)),
            dma((n_z, chunks)),
            dma((n_z, chunks)),
            dma((n_z, chunks)),
            dma((2, n_z, chunks)),
            dma((2, some)),
            dma((2, some)),
        ],
        compiler_params=pltpu.CompilerParams(
            collective_id=0, has_side_effects=True, vmem_limit_bytes=56 * 2**20
        ),
        name="conv_project",
    )(q, k, v, og, mr, rates.T, res.T, w)


def solution(mesh):
    placed = (
        P("tp", "ctx"),
        P("tp", "ctx"),
        P("tp", "ctx"),
        P("tp", "ctx"),
        P("tp", None),
        P("tp", None),
        P("tp", None),
        P("tp", None),
    )
    return jax.shard_map(
        functools.partial(per_device, mesh.shape["ctx"], mesh.shape["tp"]),
        mesh=mesh,
        in_specs=placed,
        out_specs=P("tp", "ctx"),
        check_vma=False,
    )
```
